32 devices in a mesh: groups: 2 (over x), dom: 8 (over z, y), panel: 2 (over core).
Axes of the slice: x: 2, y: 2, z: 4, core: 2. Of those that a mesh axis runs over, the one named last changes fastest.
Arguments:
- panels: float32 [8, 8192], P(None, ('groups', 'panel')), parts along dimension 1, may hold values from -1 to 1
- particles: float32 [6, 131072], P(None, ('groups', 'dom', 'panel')), parts along dimension 1, may hold values from -1 to 1
- counts: int32 [1024], P(('groups', 'dom', 'panel')), parts along dimension 0, may hold values from 1 to 128, as said below
- near: int32 [64, 512], P(('groups', 'panel'), 'dom'), parts along dimension 0, may hold values from 0 to 1, as said below
Outputs:
- normal_velocity: float32 [8192], P(('groups', 'panel')), parts along dimension 0
- particle_velocity: float32 [3, 131072], P(None, ('groups', 'dom', 'panel')), parts along dimension 1
The draws below stay inside these ranges and needn't reach their ends.
There are 2 independent parts, one for each index of `groups`. The reference program is written for one: setup_inputs(seed, part) draws one part's arguments, and reference() takes and returns one part's arrays. A program takes and returns all parts, laid end to end along the dimension named above; each array names one. Nothing has to cross between parts.
Inputs may be any that keep to these rules, and one draw needn't show every extreme that they name: `counts`: at least one block is full in every draw. Every particle block has one to three near panel blocks, adjacent to one another; there is no bound on how many particle blocks one panel block pairs with.
All inputs are finite; a program needn't handle non-finite values.
Results may differ from the reference program's by a relative error of at most 0.0003.
Values sent between devices are 32-bit elements; how exact they have to be, the bound alone decides.
No kernel may reach another device: no remote copies, remote signals or barrier semaphores. Data moves between devices by JAX's collectives and lax.ppermute only.
A program may use at most 64 MiB of HBM per device.

```python
import jax
import jax.numpy as jnp
from jax import lax

BLK = 128
NPAN = 4096
NPART = 65536
PBLK = 32
QBLK = 512


def draw_counts(key, part):
    first, second = jax.random.split(jax.random.fold_in(key, 11))
    values = jax.random.randint(first, (QBLK,), 1, BLK + 1)
    spot = jax.random.randint(second, (), 0, QBLK)
    return jnp.where(jnp.arange(QBLK) == spot, BLK, values).astype(jnp.int32)


def draw_near(key, part):
    first, second = jax.random.split(jax.random.fold_in(key, 23))
    column = jnp.arange(QBLK, dtype=jnp.int32)
    center = column * PBLK // QBLK
    back = jax.random.randint(first, (QBLK,), 0, 2)
    span = jax.random.randint(second, (QBLK,), 1, 4)
    lower = jnp.clip(center - back, 0, PBLK - 1)
    upper = jnp.minimum(lower + span, PBLK)
    row = jnp.arange(PBLK, dtype=jnp.int32)[:, None]
    return ((row >= lower[None, :]) & (row < upper[None, :])).astype(jnp.int32)


def level_of(stream_key, extent, cuts, smallest, high):
    def one(position, blocks):
        steps = jax.random.uniform(jax.random.fold_in(jax.random.fold_in(stream_key, 6), position), (blocks,), jnp.float32, smallest / len(cuts), high / len(cuts))
        return jnp.repeat(jnp.exp(steps), extent[position] // blocks).reshape((-1,) + (1,) * (len(extent) - position - 1))

    loudness = one(*cuts[0])
    for cut in cuts[1:]:
        loudness = loudness * one(*cut)
    return loudness


def setup_inputs(seed: int = 0, part: int = 0) -> dict:
    key_of = jax.random.split(jax.random.key(seed), 5)
    own_keys = jax.random.split(jax.random.fold_in(key_of[4], part), 5)
    return {
        "panels": jnp.clip(jax.random.uniform(own_keys[0], (8, NPAN), jnp.float32, -1.0, 1.0) * level_of(own_keys[0], (8, NPAN), ((1, 2),), -0.4, 0.0), -1.0, 1.0),
        "particles": jnp.clip(jax.random.uniform(own_keys[1], (6, NPART), jnp.float32, -1.0, 1.0) * level_of(own_keys[1], (6, NPART), ((1, 16),), -0.4, 0.0), -1.0, 1.0),
        "counts": draw_counts(jax.random.fold_in(jax.random.fold_in(key_of[4], part), 71), part),
        "near": draw_near(jax.random.fold_in(jax.random.fold_in(key_of[4], part), 71), part),
    }


core_sq = 0.04
inv_four_pi = 0.07957747154594767

def tile_terms(panels, pos, alpha, weight, valid):
    r = panels[0:3][:, :, None] - pos[:, None, :]
    normal = panels[3:6][:, :, None]
    source = panels[6][:, None]
    doublet = panels[7][:, None]
    inv = lax.rsqrt(lax.optimization_barrier(jnp.sum(r * r, axis=0)) + core_sq)
    inv3 = inv * inv * inv
    inv5 = inv3 * inv * inv
    av = alpha[:, None, :]
    cross0 = r[1] * av[2] - r[2] * av[1]
    cross1 = r[2] * av[0] - r[0] * av[2]
    cross2 = r[0] * av[1] - r[1] * av[0]
    ndot = normal[0] * cross0 + normal[1] * cross1 + normal[2] * cross2
    panel_part = -inv_four_pi * lax.optimization_barrier(jnp.sum(ndot * inv3 * weight * valid[None, :], axis=1))
    nr = lax.optimization_barrier(jnp.sum(normal * r, axis=0))
    coef_r = (-source * inv3 + 3.0 * doublet * nr * inv5) * weight
    coef_n = -doublet * inv3 * weight
    vel = inv_four_pi * (lax.optimization_barrier(jnp.sum(coef_r[None] * r, axis=1)) + lax.optimization_barrier(jnp.sum(normal * coef_n[None], axis=1)))
    return (panel_part, vel)

def reference(panels, particles, counts, near):
    npan = panels.shape[1]
    nblk = counts.shape[0]
    blk = particles.shape[1] // nblk
    blocks = particles.reshape(6, nblk, blk).transpose(1, 0, 2)

    def step(total, item):
        block, count, column = item
        weight = jnp.repeat(column.astype(jnp.float32), blk)[:, None]
        valid = (jnp.arange(blk, dtype=jnp.int32) < count).astype(jnp.float32)
        part, vel = tile_terms(panels, block[0:3], block[3:6], weight, valid)
        return (total + part, vel)
    total, vels = lax.scan(step, jnp.zeros((npan,), jnp.float32), (blocks, counts, near.T))
    return (total, vels.transpose(1, 0, 2).reshape(3, nblk * blk))
```

```python
import functools

import jax
import jax.numpy as jnp
from jax import lax
from jax.experimental import pallas as pl
from jax.experimental.pallas import tpu as pltpu
from jax.sharding import PartitionSpec as P

core_sq = 0.04
inv_four_pi = 0.07957747154594767
BLK = 128
WIN = 3
bf16 = jnp.bfloat16
f32 = jnp.float32


def split2(v):
    hi = v.astype(bf16)
    lo = (v - hi.astype(f32)).astype(bf16)
    return hi, lo


def split3(v):
    a = v.astype(bf16).astype(f32)
    rest = v - a
    b = rest.astype(bf16).astype(f32)
    return a, b, rest - b


def up(v, k):
    return pltpu.roll(v, (8 - k) % 8, 0)


def rows8(width):
    return lax.broadcasted_iota(jnp.int32, (8, width), 0)


def particle_features(particles, counts, ut, fe, org, tile):
    nblk = particles.shape[1] // BLK
    row = rows8(BLK)
    lane = lax.broadcasted_iota(jnp.int32, (8, BLK), 1)

    def one(q, carry):
        at = pl.ds(pl.multiple_of(q * BLK, BLK), BLK)
        t = tile.at[q % 2]
        t[0:6, :] = particles[:, at]
        p = jnp.where(row < 6, t[...], 0.0)
        x = jnp.where(row < 3, p, 0.0)
        a = jnp.where(row < 3, up(p, 3), 0.0)
        xx = jnp.sum(x * x, axis=0, keepdims=True) + core_sq
        feat = jnp.where(row < 3, x, jnp.where(row < 6, 1.0, jnp.where(row == 6, xx, 0.0)))
        x1, x2, x3 = split3(feat)
        u = jnp.concatenate([x1, x1, x2, x2, x1, x3], axis=0)
        ut[pl.ds(pl.multiple_of(q * BLK, BLK), BLK), :] = u.T.astype(bf16)
        o = jnp.broadcast_to(x[:, 0:1], (8, BLK))
        d = x - o

        def rot1(v):
            return jnp.where(row < 2, up(v, 1), jnp.where(row == 2, up(v, 6), 0.0))

        def rot2(v):
            return jnp.where(row < 1, up(v, 2), jnp.where(row < 3, up(v, 7), 0.0))

        cross = rot1(d) * rot2(a) - rot2(d) * rot1(a)
        f = jnp.where(row < 3, a, up(cross, 5))
        f = jnp.where((row < 6) & (lane < counts[q]), f, 0.0)
        f1 = f.astype(bf16).astype(f32)
        f16 = jnp.concatenate([f1, f - f1], axis=0).astype(bf16)
        fe[pl.ds(pl.multiple_of(q * 16, 16), 16), :] = jnp.concatenate([f16, f16], axis=1)
        org[pl.ds(pl.multiple_of(q * 24, 8), 8), :] = o
        org[pl.ds(pl.multiple_of(q * 24 + 8, 8), 8), :] = rot1(o)
        org[pl.ds(pl.multiple_of(q * 24 + 16, 8), 8), :] = rot2(o)
        return carry

    lax.fori_loop(0, nblk, one, 0, unroll=4)


def spans(mine, other, me, box, table, sem):
    half, cols = mine.shape
    row = lax.broadcasted_iota(jnp.int32, (half, cols), 0)
    big = jnp.int32(2 * half)
    a, b = mine[...], other[...]
    first = jnp.minimum(
        jnp.min(jnp.where(a > 0, row + me * half, big), axis=0, keepdims=True),
        jnp.min(jnp.where(b > 0, row + (1 - me) * half, big), axis=0, keepdims=True),
    )
    number = jnp.sum(a, axis=0, keepdims=True) + jnp.sum(b, axis=0, keepdims=True)
    pad = jnp.zeros((1, BLK - cols), jnp.int32) if cols < BLK else None
    if pad is not None:
        first = jnp.concatenate([first, pad], axis=1)
        number = jnp.concatenate([number, pad], axis=1)
    wide = first.shape[1]
    rowb = rows8(wide)
    box[...] = jnp.where(rowb == 0, first, jnp.where(rowb == 1, number, 0))
    return pltpu.make_async_copy(box, table, sem)


def stack6(v, c1, c2, c3, at):
    pair = jnp.concatenate([c1, c2], axis=0).astype(bf16)
    v[0:16, at] = pair
    v[16:32, at] = pair
    v[32:48, at] = jnp.concatenate([c3, c1], axis=0).astype(bf16)


def distance_rows(p, row):
    c = jnp.where(row < 3, p, 0.0)
    return jnp.where(row < 3, -2.0 * c, jnp.where(row < 6, up(c * c, 5), jnp.where(row == 6, 1.0, 0.0)))


def each_panel_chunk(panels, others, me, chunk, body):
    half = panels.shape[1]

    def run(ref, start):
        def one(k, carry):
            src = pl.ds(pl.multiple_of(k * chunk, chunk), chunk)
            dst = pl.ds(pl.multiple_of(start + k * chunk, chunk), chunk)
            body(ref[:, src], dst)
            return carry

        lax.fori_loop(0, half // chunk, one, 0, unroll=2)

    run(panels, me * half)
    run(others, (1 - me) * half)
    body(jnp.zeros((8, chunk), f32), pl.ds(2 * half, chunk))


def panel_sums(panels, others, near, near_o, ut, fe, org, out, v, n1, n2, c1, c2, tot, box, table, sem):
    me = lax.axis_index("panel")
    nblk = ut.shape[0] // BLK
    npan = 2 * panels.shape[1]
    copy = spans(near, near_o, me, box, table, sem)
    copy.start()
    chunk = 2 * BLK
    row = rows8(chunk)

    def build(p, at):
        stack6(v, *split3(distance_rows(p, row)), at)
        n1[:, at] = jnp.where(row < 2, up(p, 4), jnp.where(row == 2, up(p, 1), jnp.where(row < 6, -p, 0.0)))
        n2[:, at] = jnp.where(row < 1, up(p, 5), jnp.where(row < 3, up(p, 2), 0.0))
        c1[:, at] = jnp.where(row < 2, up(p, 1), jnp.where(row == 2, up(p, 6), 0.0))
        c2[:, at] = jnp.where(row < 1, up(p, 2), jnp.where(row < 3, up(p, 7), 1.0))
        tot[:, at] = jnp.zeros((8, chunk), f32)

    each_panel_chunk(panels, others, me, chunk, build)
    copy.wait()

    def one(q, carry):
        first = table[0, me * nblk + q]
        number = table[1, me * nblk + q]
        base = pl.multiple_of(first * BLK, BLK)
        at = pl.ds(base, WIN * BLK)
        r2 = jnp.dot(ut[pl.ds(pl.multiple_of(q * BLK, BLK), BLK), :], v[:, at], preferred_element_type=f32)
        inv = lax.rsqrt(r2)
        hi, lo = split2(inv * inv * inv)
        g = jnp.dot(
            fe[pl.ds(pl.multiple_of(q * 16, 16), 16), :],
            jnp.concatenate([hi, lo], axis=0),
            preferred_element_type=f32,
        )
        g = g[0:8] + g[8:16]
        o1 = org[pl.ds(pl.multiple_of(q * 24 + 8, 8), 8), :]
        o2 = org[pl.ds(pl.multiple_of(q * 24 + 16, 8), 8), :]
        for k in range(WIN):
            here = pl.ds(pl.multiple_of(base + k * BLK, BLK), BLK)
            m = n1[:, here] * (c2[:, here] - o2) - n2[:, here] * (c1[:, here] - o1)
            add = g[:, k * BLK : (k + 1) * BLK] * m
            tot[:, here] += jnp.where(k < number, add, 0.0)
        return carry

    lax.fori_loop(0, nblk, one, 0, unroll=4)
    out[...] = -inv_four_pi * jnp.sum(tot[:, 0:npan], axis=0, keepdims=True)


def particle_sums(particles, panels, others, near, near_o, ut, org, out, v, vn, d0, sb, mn, tile, box, table, sem):
    me = lax.axis_index("panel")
    nblk = ut.shape[0] // BLK
    copy = spans(near, near_o, me, box, table, sem)
    copy.start()
    chunk = 2 * BLK
    row = rows8(chunk)

    def build(p, at):
        stack6(v, *split3(distance_rows(p, row)), at)
        n = up(p, 3)
        m = jnp.broadcast_to(p[7:8, :], p.shape)
        mn3 = jnp.where(row < 3, n * m, 0.0)
        c = jnp.where(row < 3, p, 0.0)
        stack6(vn, *split3(jnp.where(row < 3, -3.0 * mn3, up(3.0 * mn3 * c, 5))), at)
        d0[:, at] = jnp.where(row < 3, p, jnp.where(row == 3, 1.0, 0.0))
        sb[:, at] = jnp.broadcast_to(p[6:7, :], p.shape)
        mn[:, at] = mn3

    each_panel_chunk(panels, others, me, chunk, build)
    copy.wait()
    dims = (((1,), (1,)), ((), ()))

    def one(q, carry):
        first = table[0, me * nblk + q]
        number = table[1, me * nblk + q]
        at = pl.ds(pl.multiple_of(first * BLK, BLK), WIN * BLK)
        mine = pl.ds(pl.multiple_of(q * BLK, BLK), BLK)
        u = ut[mine, :]
        r2 = jnp.dot(u, v[:, at], preferred_element_type=f32)
        nr = jnp.dot(u, vn[:, at], preferred_element_type=f32)
        inv = lax.rsqrt(r2)
        inv2 = inv * inv
        inv3 = inv2 * inv
        term = inv3 * (inv2 * nr)
        o = org[pl.ds(pl.multiple_of(q * 24, 8), 8), :]
        wide = jnp.concatenate([o] * WIN, axis=1)
        lane = lax.broadcasted_iota(jnp.int32, (8, WIN * BLK), 1)
        live = lane < number * BLK
        d = jnp.where(live, d0[:, at] - wide, 0.0)
        e = jnp.where(live, -sb[:, at] * d - mn[:, at], 0.0)

        def rows16(w):
            w1 = w.astype(bf16).astype(f32)
            return jnp.concatenate([w1, w - w1], axis=0).astype(bf16)

        d16, e16 = rows16(d), rows16(e)
        t1, t2 = split2(term)
        i1, i2 = split2(inv3)
        h = (
            lax.dot_general(d16, t1, dims, preferred_element_type=f32)
            + lax.dot_general(d16, t2, dims, preferred_element_type=f32)
            + lax.dot_general(e16, i1, dims, preferred_element_type=f32)
            + lax.dot_general(e16, i2, dims, preferred_element_type=f32)
        )
        h = h[0:8] + h[8:16]
        x = particles[0:3, mine] - o[0:3]
        out[:, mine] = inv_four_pi * (h[0:3] - x * h[3:4])
        return carry

    lax.fori_loop(0, nblk, one, 0, unroll=2)


def vmem():
    return pl.BlockSpec(memory_space=pltpu.VMEM)


def smem():
    return pl.BlockSpec(memory_space=pltpu.SMEM)


def params():
    return pltpu.CompilerParams(vmem_limit_bytes=24 * 1024 * 1024)


def prepare(particles, counts):
    width = particles.shape[1]
    nblk = width // BLK
    return pl.pallas_call(
        particle_features,
        out_shape=(
            jax.ShapeDtypeStruct((width, 48), bf16),
            jax.ShapeDtypeStruct((nblk * 16, 2 * BLK), bf16),
            jax.ShapeDtypeStruct((nblk * 24, BLK), f32),
        ),
        in_specs=[vmem(), smem()],
        out_specs=(vmem(), vmem(), vmem()),
        scratch_shapes=[pltpu.VMEM((2, 8, BLK), f32)],
        compiler_params=params(),
        name="prepare",
    )(particles, counts)


def table_scratch(cols):
    wide = max(cols, BLK)
    return [pltpu.VMEM((8, wide), jnp.int32), pltpu.SMEM((8, wide), jnp.int32), pltpu.SemaphoreType.DMA]


def panel_side(panels, others, near, near_o, ut, fe, org):
    npan = 2 * panels.shape[1]
    full = npan + 2 * BLK
    return pl.pallas_call(
        panel_sums,
        out_shape=jax.ShapeDtypeStruct((1, npan), f32),
        in_specs=[vmem()] * 7,
        out_specs=vmem(),
        scratch_shapes=[pltpu.VMEM((48, full), bf16)]
        + [pltpu.VMEM((8, full), f32)] * 5
        + table_scratch(near.shape[1]),
        compiler_params=params(),
        name="panel_side",
    )(panels, others, near, near_o, ut, fe, org)


def particle_side(particles, panels, others, near, near_o, ut, org):
    npan = 2 * panels.shape[1]
    full = npan + 2 * BLK
    return pl.pallas_call(
        particle_sums,
        out_shape=jax.ShapeDtypeStruct((3, particles.shape[1]), f32),
        in_specs=[vmem()] * 7,
        out_specs=vmem(),
        scratch_shapes=[pltpu.VMEM((48, full), bf16)] * 2
        + [pltpu.VMEM((8, full), f32)] * 3
        + [pltpu.VMEM((8, BLK), f32)]
        + table_scratch(near.shape[1]),
        compiler_params=params(),
        name="particle_side",
    )(particles, panels, others, near, near_o, ut, org)


def on_device(dom, panels, particles, counts, near):
    swap = [(0, 1), (1, 0)]
    others = lax.ppermute(panels, "panel", swap)
    near_o = lax.ppermute(near, "panel", swap)
    ut, fe, org = prepare(particles, counts)
    total = panel_side(panels, others, near, near_o, ut, fe, org)
    velocity = particle_side(particles, panels, others, near, near_o, ut, org)
    total = total.reshape(total.shape[1])
    step = 1
    while step < dom:
        pairs = [(2 * i + c, 2 * (i ^ step) + 1 - c) for i in range(dom) for c in range(2)]
        total = total + lax.ppermute(total, ("dom", "panel"), pairs)
        step *= 2
    half = total.shape[0] // 2
    me = lax.axis_index("panel")
    keep = lax.dynamic_slice(total, (me * half,), (half,))
    give = lax.dynamic_slice(total, ((1 - me) * half,), (half,))
    return keep + lax.ppermute(give, "panel", swap), velocity


def solution(mesh):
    return jax.shard_map(
        functools.partial(on_device, mesh.shape["dom"]),
        mesh=mesh,
        in_specs=(
            P(None, ("groups", "panel")),
            P(None, ("groups", "dom", "panel")),
            P(("groups", "dom", "panel")),
            P(("groups", "panel"), "dom"),
        ),
        out_specs=(P(("groups", "panel")), P(None, ("groups", "dom", "panel"))),
        check_vma=False,
    )
```

```python
import functools

import jax
import jax.numpy as jnp
from jax import lax
from jax.experimental import pallas as pl
from jax.experimental.pallas import tpu as pltpu
from jax.sharding import PartitionSpec as P

core_sq = 0.04
inv_four_pi = 0.07957747154594767
BLK = 128
WIN = 3
EACH1 = 16
EACH = 8
bf16 = jnp.bfloat16
f32 = jnp.float32


def split2(v):
    hi = v.astype(bf16)
    lo = (v - hi.astype(f32)).astype(bf16)
    return hi, lo


def split3(v):
    a = v.astype(bf16).astype(f32)
    rest = v - a
    b = rest.astype(bf16).astype(f32)
    return a, b, rest - b


def rows16(w):
    w1 = w.astype(bf16).astype(f32)
    return jnp.concatenate([w1, w - w1], axis=0).astype(bf16)


def up(v, k):
    return pltpu.roll(v, (8 - k) % 8, 0)


def rows8(width):
    return lax.broadcasted_iota(jnp.int32, (8, width), 0)


def block(q, size):
    return pl.ds(pl.multiple_of(q * size, size), size)


def particle_features(particles, u_t, u_n, fe, org, parts):
    nblk = particles.shape[1] // BLK
    parts[0:6, :] = particles[...]
    row = rows8(BLK)

    def one(q, carry):
        p = parts[:, block(q, BLK)]
        x = jnp.where(row < 3, p, 0.0)
        a = jnp.where(row < 3, up(p, 3), 0.0)
        xx = jnp.sum(x * x, axis=0, keepdims=True) + core_sq
        feat = jnp.where(row < 3, x, jnp.where(row < 6, 1.0, jnp.where(row == 6, xx, 0.0)))
        x1, x2, x3 = split3(feat)
        u = jnp.concatenate([x1, x1, x2, x2, x1, x3], axis=0)
        u_t[block(q, BLK), :] = u.T.astype(bf16)
        u_n[:, block(q, BLK)] = u.astype(bf16)
        o = jnp.broadcast_to(x[:, 0:1], (8, BLK))
        d = x - o

        def rot1(v):
            return jnp.where(row < 2, up(v, 1), jnp.where(row == 2, up(v, 6), 0.0))

        def rot2(v):
            return jnp.where(row < 1, up(v, 2), jnp.where(row < 3, up(v, 7), 0.0))

        cross = rot1(d) * rot2(a) - rot2(d) * rot1(a)
        f = jnp.where(row < 3, a, up(cross, 5))
        f = jnp.where(row < 6, f, 0.0)
        f16 = rows16(f)
        fe[block(q, 16), :] = jnp.concatenate([f16, f16], axis=1)
        for i, v in enumerate((o, rot1(o), rot2(o), d)):
            org[pl.ds(pl.multiple_of(q * 32 + 8 * i, 8), 8), :] = v
        return carry

    lax.fori_loop(0, nblk, one, 0, unroll=4)


def spans(mine, other, me, box):
    half, cols = mine.shape
    row = lax.broadcasted_iota(jnp.int32, (half, cols), 0)
    big = jnp.int32(2 * half)
    a, b = mine[...], other[...]
    first = jnp.minimum(
        jnp.min(jnp.where(a > 0, row + me * half, big), axis=0, keepdims=True),
        jnp.min(jnp.where(b > 0, row + (1 - me) * half, big), axis=0, keepdims=True),
    )
    number = jnp.sum(a, axis=0, keepdims=True) + jnp.sum(b, axis=0, keepdims=True)
    if cols < BLK:
        pad = jnp.zeros((1, BLK - cols), jnp.int32)
        first = jnp.concatenate([first, pad], axis=1)
        number = jnp.concatenate([number, pad], axis=1)
    rowb = rows8(first.shape[1])
    box[...] = jnp.where(rowb == 0, first, jnp.where(rowb == 1, number, 0))


def each_panel_chunk(panels, others, me, chunk, body):
    half = panels.shape[1]

    def run(ref, start):
        def one(k, carry):
            src = pl.ds(pl.multiple_of(k * chunk, chunk), chunk)
            dst = pl.ds(pl.multiple_of(start + k * chunk, chunk), chunk)
            body(ref[:, src], dst)
            return carry

        lax.fori_loop(0, half // chunk, one, 0, unroll=2)

    run(panels, me * half)
    run(others, (1 - me) * half)
    body(jnp.zeros((8, chunk), f32), pl.ds(2 * half, chunk))


def stack6(v, c1, c2, c3, at):
    pair = jnp.concatenate([c1, c2], axis=0).astype(bf16)
    v[0:16, at] = pair
    v[16:32, at] = pair
    v[32:48, at] = jnp.concatenate([c3, c1], axis=0).astype(bf16)


def list_items(table, offset, count, items):
    filled = jnp.int32(0)
    for i in range(count):
        first = table[0, offset + i]
        number = table[1, offset + i]
        for k in range(WIN):
            items[0, filled] = i
            items[1, filled] = first + k
            filled = filled + jnp.where(k < number, 1, 0)
    return filled


def panel_sums(counts, panels, others, near, near_o, ut, fe, org, out, pan, box, v, n1, n2, c1, c2, tot, table, items, sem):
    me = lax.axis_index("panel")
    nblk = ut.shape[0] // BLK
    npan = 2 * panels.shape[1]
    spans(near, near_o, me, box)
    copy = pltpu.make_async_copy(box, table, sem)
    copy.start()
    chunk = 2 * BLK
    row = rows8(chunk)

    def build(p, at):
        pan[:, at] = p
        c = jnp.where(row < 3, p, 0.0)
        dist = jnp.where(row < 3, -2.0 * c, jnp.where(row < 6, up(c * c, 5), jnp.where(row == 6, 1.0, 0.0)))
        stack6(v, *split3(dist), at)
        n1[:, at] = jnp.where(row < 2, up(p, 4), jnp.where(row == 2, up(p, 1), jnp.where(row < 6, -p, 0.0)))
        n2[:, at] = jnp.where(row < 1, up(p, 5), jnp.where(row < 3, up(p, 2), 0.0))
        c1[:, at] = jnp.where(row < 2, up(p, 1), jnp.where(row == 2, up(p, 6), 0.0))
        c2[:, at] = jnp.where(row < 1, up(p, 2), jnp.where(row < 3, up(p, 7), 1.0))
        tot[:, at] = jnp.zeros((8, chunk), f32)

    each_panel_chunk(panels, others, me, chunk, build)
    copy.wait()

    filled = list_items(table, me * nblk, nblk, items)
    lane = lax.broadcasted_iota(jnp.int32, (16, 2 * BLK), 1) % BLK

    def moments(n):
        q, at = items[0, n], block(items[1, n], BLK)
        r2 = jnp.dot(ut[block(q, BLK), :], v[:, at], preferred_element_type=f32)
        inv = lax.rsqrt(r2)
        hi, lo = split2(inv * inv * inv)
        weight = jnp.where(lane < counts[q], 1.0, 0.0).astype(bf16)
        return fe[block(q, 16), :] * weight, jnp.concatenate([hi, lo], axis=0)

    def finish(n, g, keep):
        q, at = items[0, n], block(items[1, n], BLK)
        o1 = org[pl.ds(pl.multiple_of(q * 32 + 8, 8), 8), :]
        o2 = org[pl.ds(pl.multiple_of(q * 32 + 16, 8), 8), :]
        m = n1[:, at] * (c2[:, at] - o2) - n2[:, at] * (c1[:, at] - o1)
        tot[:, at] += (g[0:8] + g[8:16]) * (m * keep)

    def some(i, carry):
        ns = [jnp.minimum(i * EACH1 + e, filled - 1) for e in range(EACH1)]
        keeps = [jnp.where(i * EACH1 + e < filled, 1.0, 0.0) for e in range(EACH1)]
        parts = [moments(n) for n in ns]
        for e in range(0, EACH1, 2):
            (fa, ka), (fb, kb) = parts[e], parts[e + 1]
            g = jnp.dot(
                jnp.concatenate([fa, fb], axis=0), jnp.concatenate([ka, kb], axis=1), preferred_element_type=f32
            )
            finish(ns[e], g[0:16, 0:BLK], keeps[e])
            finish(ns[e + 1], g[16:32, BLK:], keeps[e + 1])
        return carry

    lax.fori_loop(0, (filled + EACH1 - 1) // EACH1, some, 0)
    out[...] = -inv_four_pi * jnp.sum(tot[:, 0:npan], axis=0, keepdims=True)


def particle_sums(start, count, nblk, build, pan, table, un, v, org, *rest):
    items = rest[-1]
    row8 = rows8(BLK)
    if build:
        out, vn = rest[:2]
        earlier = []
        chunk = 2 * BLK
        row = rows8(chunk)

        def one_chunk(k, carry):
            at = block(k, chunk)
            p = pan[:, at]
            mn3 = jnp.where(row < 3, up(p, 3) * p[7:8, :], 0.0) * 3.0
            c = jnp.where(row < 3, p, 0.0)
            stack6(vn, *split3(jnp.where(row < 3, -mn3, up(mn3 * c, 5))), at)
            return carry

        lax.fori_loop(0, pan.shape[1] // chunk, one_chunk, 0)
    else:
        vn = rest[0]
        earlier, out = rest[1:-2], rest[-2]
    me = lax.axis_index("panel")
    offset = 0
    for e in earlier:
        out[:, offset : offset + e.shape[1]] = e[...]
        offset += e.shape[1]
    out[:, offset : offset + count * BLK] = jnp.zeros((3, count * BLK), f32)
    filled = list_items(table, me * nblk + start, count, items)
    turn = (((0,), (0,)), ((), ()))

    def factors(n):
        i, at = items[0, n], block(items[1, n], BLK)
        q = start + i
        p = pan[:, at]
        d = jnp.where(row8 < 3, p - org[pl.ds(pl.multiple_of(q * 32, 8), 8), :], jnp.where(row8 == 3, 1.0, 0.0))
        mn = jnp.where(row8 < 3, up(p, 3) * p[7:8], 0.0)
        d16, e16 = rows16(d), rows16(-p[6:7] * d - mn)
        u = un[:, block(q, BLK)]
        r2 = lax.dot_general(v[:, at], u, turn, preferred_element_type=f32)
        nr = lax.dot_general(vn[:, at], u, turn, preferred_element_type=f32)
        inv = lax.rsqrt(r2)
        inv2 = inv * inv
        inv3 = inv2 * inv
        t1, t2 = split2(inv3 * (inv2 * nr))
        i1, i2 = split2(inv3)
        return jnp.concatenate([d16, d16, e16, e16], axis=1), jnp.concatenate([t1, t2, i1, i2], axis=0)

    def finish(n, h, keep):
        i = items[0, n]
        x = org[pl.ds(pl.multiple_of((start + i) * 32 + 24, 8), 8), :]
        h = (h[0:8] + h[8:16]) * keep
        out[:, pl.ds(pl.multiple_of(offset + i * BLK, BLK), BLK)] += h[0:3] - x[0:3] * h[3:4]

    def some(i, carry):
        ns = [jnp.minimum(i * EACH + e, filled - 1) for e in range(EACH)]
        keeps = [jnp.where(i * EACH + e < filled, inv_four_pi, 0.0) for e in range(EACH)]
        parts = [factors(n) for n in ns]
        for e in range(0, EACH, 2):
            (fa, ka), (fb, kb) = parts[e], parts[e + 1]
            h = jnp.dot(
                jnp.concatenate([fa, fb], axis=0), jnp.concatenate([ka, kb], axis=1), preferred_element_type=f32
            )
            finish(ns[e], h[0:16, 0:BLK], keeps[e])
            finish(ns[e + 1], h[16:32, BLK:], keeps[e + 1])
        return carry

    lax.fori_loop(0, (filled + EACH - 1) // EACH, some, 0)


def vmem():
    return pl.BlockSpec(memory_space=pltpu.VMEM)


def smem():
    return pl.BlockSpec(memory_space=pltpu.SMEM)


def params(mib=24):
    return pltpu.CompilerParams(vmem_limit_bytes=mib * 1024 * 1024)


def prepare(particles):
    width = particles.shape[1]
    nblk = width // BLK
    return pl.pallas_call(
        particle_features,
        out_shape=(
            jax.ShapeDtypeStruct((width, 48), bf16),
            jax.ShapeDtypeStruct((48, width), bf16),
            jax.ShapeDtypeStruct((nblk * 16, 2 * BLK), bf16),
            jax.ShapeDtypeStruct((nblk * 32, BLK), f32),
        ),
        in_specs=[vmem()],
        out_specs=(vmem(),) * 4,
        scratch_shapes=[pltpu.VMEM((8, width), f32)],
        compiler_params=params(),
        name="prepare",
    )(particles)


def panel_side(counts, panels, others, near, near_o, ut, fe, org):
    npan = 2 * panels.shape[1]
    full = npan + 2 * BLK
    wide = max(near.shape[1], BLK)
    return pl.pallas_call(
        panel_sums,
        out_shape=(
            jax.ShapeDtypeStruct((1, npan), f32),
            jax.ShapeDtypeStruct((8, full), f32),
            jax.ShapeDtypeStruct((8, wide), jnp.int32),
            jax.ShapeDtypeStruct((48, full), bf16),
        ),
        in_specs=[smem()] + [vmem()] * 7,
        out_specs=(vmem(),) * 4,
        scratch_shapes=[pltpu.VMEM((8, full), f32)] * 5
        + [
            pltpu.SMEM((8, wide), jnp.int32),
            pltpu.SMEM((2, WIN * counts.shape[0] + 1), jnp.int32),
            pltpu.SemaphoreType.DMA,
        ],
        compiler_params=params(),
        name="panel_side",
    )(counts, panels, others, near, near_o, ut, fe, org)


def particle_side(start, count, nblk, pan, box, un, v, org, vn, earlier):
    done = sum(e.shape[1] for e in earlier)
    build = vn is None
    shape = jax.ShapeDtypeStruct((3, done + count * BLK), f32)
    args = [pan, box, un, v, org] + ([] if build else [vn]) + list(earlier)
    return pl.pallas_call(
        functools.partial(particle_sums, start, count, nblk, build),
        out_shape=(shape, jax.ShapeDtypeStruct(v.shape, bf16)) if build else shape,
        in_specs=[vmem(), smem()] + [vmem()] * (len(args) - 2),
        out_specs=(vmem(), vmem()) if build else vmem(),
        scratch_shapes=[pltpu.SMEM((2, WIN * count + 1), jnp.int32)],
        compiler_params=params(),
        cost_estimate=pl.CostEstimate(flops=count * 3 * BLK * BLK * 32, bytes_accessed=count * 1000, transcendentals=0),
        name="particle_side",
    )(*args)


def on_device(dom, panels, particles, counts, near):
    swap = [(0, 1), (1, 0)]
    others = lax.ppermute(panels, "panel", swap)
    near_o = lax.ppermute(near, "panel", swap)
    ut, un, fe, org = prepare(particles)
    total, pan, box, v = panel_side(counts, panels, others, near, near_o, ut, fe, org)
    total = total.reshape(total.shape[1])
    nblk = counts.shape[0]
    steps = [1 << b for b in range((dom - 1).bit_length())]
    edges = [nblk * i // (len(steps) + 1) for i in range(len(steps) + 2)]
    chunks, factors = [], None

    for number, step in enumerate(steps):
        pairs = [(2 * i + c, 2 * (i ^ step) + 1 - c) for i in range(dom) for c in range(2)]
        total, at = lax.optimization_barrier((total, box))
        got = particle_side(edges[number], edges[number + 1] - edges[number], nblk, pan, at, un, v, org, factors, [])
        if factors is None:
            got, factors = got
        arrived, got = lax.optimization_barrier((lax.ppermute(total, ("dom", "panel"), pairs), got))
        chunks.append(got)
        total = total + arrived
    half = total.shape[0] // 2
    me = lax.axis_index("panel")
    total, at = lax.optimization_barrier((total, box))
    velocity = particle_side(edges[-2], edges[-1] - edges[-2], nblk, pan, at, un, v, org, factors, chunks)
    keep = lax.dynamic_slice(total, (me * half,), (half,))
    give = lax.dynamic_slice(total, ((1 - me) * half,), (half,))
    return keep + lax.ppermute(give, "panel", swap), velocity


def solution(mesh):
    return jax.shard_map(
        functools.partial(on_device, mesh.shape["dom"]),
        mesh=mesh,
        in_specs=(
            P(None, ("groups", "panel")),
            P(None, ("groups", "dom", "panel")),
            P(("groups", "dom", "panel")),
            P(("groups", "panel"), "dom"),
        ),
        out_specs=(P(("groups", "panel")), P(None, ("groups", "dom", "panel"))),
        check_vma=False,
    )
```

```python
import functools

import jax
import jax.numpy as jnp
from jax import lax
from jax.experimental import pallas as pl
from jax.experimental.pallas import tpu as pltpu
from jax.sharding import PartitionSpec as P

core_sq = 0.04
inv_four_pi = 0.07957747154594767
BLK = 128
WIN = 3
EACH1 = 16
EACH = 8
bf16 = jnp.bfloat16
f32 = jnp.float32


def split2(v):
    hi = v.astype(bf16)
    lo = (v - hi.astype(f32)).astype(bf16)
    return hi, lo


def split3(v):
    a = v.astype(bf16).astype(f32)
    rest = v - a
    b = rest.astype(bf16).astype(f32)
    return a, b, rest - b


def rows16(w):
    w1 = w.astype(bf16).astype(f32)
    return jnp.concatenate([w1, w - w1], axis=0).astype(bf16)


def up(v, k):
    return pltpu.roll(v, (8 - k) % 8, 0)


def rows8(width):
    return lax.broadcasted_iota(jnp.int32, (8, width), 0)


def block(q, size):
    return pl.ds(pl.multiple_of(q * size, size), size)


def particle_features(particles, un, fe, org, parts):
    nblk = particles.shape[1] // BLK
    parts[0:6, :] = particles[...]
    row = rows8(BLK)

    def one(q, carry):
        p = parts[:, block(q, BLK)]
        x = jnp.where(row < 3, p, 0.0)
        a = jnp.where(row < 3, up(p, 3), 0.0)
        xx = jnp.sum(x * x, axis=0, keepdims=True) + core_sq
        feat = jnp.where(row < 3, x, jnp.where(row < 6, 1.0, jnp.where(row == 6, xx, 0.0)))
        x1, x2, x3 = split3(feat)
        u = jnp.concatenate([x1, x1, x2, x2, x1, x3], axis=0)
        un[q] = u.astype(bf16)
        o = jnp.broadcast_to(x[:, 0:1], (8, BLK))
        d = x - o

        def rot1(v):
            return jnp.where(row < 2, up(v, 1), jnp.where(row == 2, up(v, 6), 0.0))

        def rot2(v):
            return jnp.where(row < 1, up(v, 2), jnp.where(row < 3, up(v, 7), 0.0))

        cross = rot1(d) * rot2(a) - rot2(d) * rot1(a)
        f = jnp.where(row < 3, a, up(cross, 5))
        f = jnp.where(row < 6, f, 0.0)
        f16 = rows16(f)
        fe[q] = jnp.concatenate([f16, f16], axis=1)
        for i, v in enumerate((o, rot1(o), rot2(o), d)):
            org[q, 8 * i : 8 * i + 8, :] = v
        return carry

    lax.fori_loop(0, nblk, one, 0, unroll=4)


def list_pairs(mine, other, counts, me, nblk, column, box):
    half, cols = mine.shape
    row = lax.broadcasted_iota(jnp.int32, (half, cols), 0)
    big = jnp.int32(2 * half)
    a, b = mine[...], other[...]
    first = jnp.minimum(
        jnp.min(jnp.where(a > 0, row + me * half, big), axis=0, keepdims=True),
        jnp.min(jnp.where(b > 0, row + (1 - me) * half, big), axis=0, keepdims=True),
    )
    number = jnp.sum(a, axis=0, keepdims=True) + jnp.sum(b, axis=0, keepdims=True)
    row8 = rows8(cols)
    alive = counts[...]
    if nblk < cols:
        alive = jnp.concatenate([alive, jnp.zeros((1, cols - nblk), jnp.int32)], axis=1)
    column[...] = jnp.where(row8 == 0, first, jnp.where(row8 == 1, number, alive)).astype(f32).T
    own = column[pl.ds(pl.multiple_of(me * nblk, 8), nblk), :]
    wide = box.shape[1]
    first = jnp.broadcast_to(own[:, 0:1], (nblk, wide))
    number = jnp.broadcast_to(own[:, 1:2], (nblk, wide))
    alive = jnp.broadcast_to(column[0:nblk, 2:3], (nblk, wide))
    before = lax.broadcasted_iota(jnp.int32, (nblk, nblk), 0) > lax.broadcasted_iota(jnp.int32, (nblk, nblk), 1)
    start = jnp.dot(before.astype(f32).astype(bf16), number.astype(bf16), preferred_element_type=f32)
    lane = lax.broadcasted_iota(jnp.int32, (nblk, wide), 1).astype(f32)
    block_of = lax.broadcasted_iota(jnp.int32, (nblk, wide), 0).astype(f32)
    here = (lane >= start) & (lane < start + number)
    particle = jnp.sum(jnp.where(here, block_of, 0.0), axis=0, keepdims=True)
    empty = 2.0 * half
    panel = empty + jnp.sum(jnp.where(here, first + lane - start - empty, 0.0), axis=0, keepdims=True)
    alive = jnp.sum(jnp.where(here, alive, 0.0), axis=0, keepdims=True)
    total = jnp.sum(number, axis=0, keepdims=True)
    row8 = rows8(wide)
    box[...] = jnp.where(row8 == 0, particle, jnp.where(row8 == 1, panel, jnp.where(row8 == 2, alive, total))).astype(jnp.int32)


def each_panel_block(panels, others, me, body):
    many = panels.shape[1] // BLK

    def run(ref, start):
        def one(k, carry):
            body(ref[:, block(k, BLK)], start + k)
            return carry

        lax.fori_loop(0, many, one, 0, unroll=4)

    run(panels, me * many)
    run(others, (1 - me) * many)
    for extra in range(WIN - 1):
        body(jnp.zeros((8, BLK), f32), 2 * many + extra)


def stack6(c1, c2, c3):
    pair = jnp.concatenate([c1, c2], axis=0).astype(bf16)
    return jnp.concatenate([pair, pair, jnp.concatenate([c3, c1], axis=0).astype(bf16)], axis=0)


def apart(a, b):
    none = jnp.zeros(a.shape, a.dtype)
    return jnp.concatenate([jnp.concatenate([a, none], axis=1), jnp.concatenate([none, b], axis=1)], axis=0)


TURN = (((0,), (0,)), ((), ()))


def panel_sums(counts, panels, others, near, near_o, un, fe, org, out, pan, box, v, geo, tot, column, items, sem):
    me = lax.axis_index("panel")
    nblk = un.shape[0]
    list_pairs(near, near_o, counts, me, nblk, column, box)
    copy = pltpu.make_async_copy(box, items, sem)
    copy.start()
    row = rows8(BLK)

    def build(p, at):
        pan[at] = p
        c = jnp.where(row < 3, p, 0.0)
        dist = jnp.where(row < 3, -2.0 * c, jnp.where(row < 6, up(c * c, 5), jnp.where(row == 6, 1.0, 0.0)))
        v[at] = stack6(*split3(dist))
        geo[at, 0:8, :] = jnp.where(row < 2, up(p, 4), jnp.where(row == 2, up(p, 1), jnp.where(row < 6, -p, 0.0)))
        geo[at, 8:16, :] = jnp.where(row < 1, up(p, 5), jnp.where(row < 3, up(p, 2), 0.0))
        geo[at, 16:24, :] = jnp.where(row < 2, up(p, 1), jnp.where(row == 2, up(p, 6), 0.0))
        geo[at, 24:32, :] = jnp.where(row < 1, up(p, 2), jnp.where(row < 3, up(p, 7), 1.0))
        tot[at] = jnp.zeros((8, BLK), f32)

    each_panel_block(panels, others, me, build)
    copy.wait()
    filled = items[3, 0]
    lane = lax.broadcasted_iota(jnp.int32, (16, 2 * BLK), 1) % BLK

    def moments(n):
        qa, qb = items[0, n], items[0, n + 1]
        u = jnp.concatenate([un[qa], un[qb]], axis=0)
        r2 = lax.dot_general(u, apart(v[items[1, n]], v[items[1, n + 1]]), TURN, preferred_element_type=f32)
        inv = lax.rsqrt(r2)
        hi, lo = split2(inv * inv * inv)
        f = [fe[q] * jnp.where(lane < items[2, n + i], 1.0, 0.0).astype(bf16) for i, q in enumerate((qa, qb))]
        return jnp.concatenate(f, axis=0), jnp.concatenate([hi, lo], axis=0)

    def finish(n, g):
        q, at = items[0, n], items[1, n]
        m = geo[at, 0:8, :] * (geo[at, 24:32, :] - org[q, 16:24, :]) - geo[at, 8:16, :] * (geo[at, 16:24, :] - org[q, 8:16, :])
        tot[at] += (g[0:8] + g[8:16]) * m

    def some(i, carry):
        ns = [i * EACH1 + e for e in range(0, EACH1, 2)]
        parts = [moments(n) for n in ns]
        for n, (f, k) in zip(ns, parts):
            g = jnp.dot(f, k, preferred_element_type=f32)
            finish(n, g[0:16, 0:BLK])
            finish(n + 1, g[16:32, BLK:])
        return carry

    lax.fori_loop(0, (filled + EACH1 - 1) // EACH1, some, 0)
    for k in range(out.shape[1] // BLK):
        out[:, k * BLK : (k + 1) * BLK] = -inv_four_pi * jnp.sum(tot[k], axis=0, keepdims=True)


def share(rounds, part, parts):
    return jnp.minimum(rounds, (2 * part * rounds + 2 * parts - 2) // (2 * parts - 1))


def particle_sums(part, parts, build, pan, items, un, v, org, *rest):
    row = rows8(BLK)
    last = part == parts - 1
    if build:
        out, vn = rest[:2]
        earlier = []

        def one_block(k, carry):
            p = pan[k]
            mn3 = jnp.where(row < 3, up(p, 3) * p[7:8, :], 0.0) * 3.0
            c = jnp.where(row < 3, p, 0.0)
            vn[k] = stack6(*split3(jnp.where(row < 3, -mn3, up(mn3 * c, 5))))
            return carry

        lax.fori_loop(0, pan.shape[0], one_block, 0, unroll=2)
    else:
        vn = rest[0]
        earlier, out = (rest[1:-2], rest[-2]) if last else (rest[1:-1], rest[-1])
    total = rest[-1] if last else out
    total[...] = sum((e[...] for e in earlier), jnp.zeros(total.shape, f32))
    listed = items[...]
    filled = listed[3, 0]
    def rows(n):
        p = pan[n[1]]
        d = jnp.where(row < 3, p - org[n[0], 0:8, :], jnp.where(row == 3, 1.0, 0.0))
        mn = jnp.where(row < 3, up(p, 3) * p[7:8], 0.0)
        d16, e16 = rows16(d), rows16(-p[6:7] * d - mn)
        return jnp.concatenate([d16, d16, e16, e16], axis=1)

    def factors(n, m):
        both = [jnp.concatenate([v[at], vn[at]], axis=1) for at in (n[1], m[1])]
        u = apart(un[n[0]], un[m[0]])
        pair = lax.dot_general(jnp.concatenate(both, axis=0), u, TURN, preferred_element_type=f32)
        inv = lax.rsqrt(pair[0:BLK])
        inv2 = inv * inv
        inv3 = inv2 * inv
        t1, t2 = split2(inv3 * (inv2 * pair[BLK:]))
        i1, i2 = split2(inv3)
        return jnp.concatenate([rows(n), rows(m)], axis=0), jnp.concatenate([t1, t2, i1, i2], axis=0)

    def finish(n, h):
        q = n[0]
        h = (h[0:8] + h[8:16]) * inv_four_pi
        total[q] += h - org[q, 24:32, :] * h[3:4]

    def some(i, carry):
        now = pltpu.roll(listed, listed.shape[1] - i * EACH, 1)
        ns = [(now[0, e], now[1, e]) for e in range(EACH)]
        parts = [factors(ns[e], ns[e + 1]) for e in range(0, EACH, 2)]
        for e, (f, k) in zip(range(0, EACH, 2), parts):
            h = jnp.dot(f, k, preferred_element_type=f32)
            finish(ns[e], h[0:16, 0:BLK])
            finish(ns[e + 1], h[16:32, BLK:])
        return carry

    rounds = (filled + EACH - 1) // EACH
    lax.fori_loop(share(rounds, part, parts), share(rounds, part + 1, parts), some, 0)
    if last:
        for q in range(total.shape[0]):
            out[:, q * BLK : (q + 1) * BLK] = total[q, 0:3, :]


def vmem():
    return pl.BlockSpec(memory_space=pltpu.VMEM)


def smem():
    return pl.BlockSpec(memory_space=pltpu.SMEM)


def params(mib=24):
    return pltpu.CompilerParams(vmem_limit_bytes=mib * 1024 * 1024)


def prepare(particles):
    width = particles.shape[1]
    nblk = width // BLK
    return pl.pallas_call(
        particle_features,
        out_shape=(
            jax.ShapeDtypeStruct((nblk, 48, BLK), bf16),
            jax.ShapeDtypeStruct((nblk, 16, 2 * BLK), bf16),
            jax.ShapeDtypeStruct((nblk, 32, BLK), f32),
        ),
        in_specs=[vmem()],
        out_specs=(vmem(),) * 3,
        scratch_shapes=[pltpu.VMEM((8, width), f32)],
        compiler_params=params(),
        cost_estimate=pl.CostEstimate(flops=2 * 10**9, bytes_accessed=10**6, transcendentals=0),
        name="prepare",
    )(particles)


def panel_side(counts, panels, others, near, near_o, un, fe, org):
    npan = 2 * panels.shape[1]
    full = npan // BLK + WIN - 1
    wide = pl.cdiv(WIN * counts.shape[1] + EACH1, BLK) * BLK
    return pl.pallas_call(
        panel_sums,
        out_shape=(
            jax.ShapeDtypeStruct((1, npan), f32),
            jax.ShapeDtypeStruct((full, 8, BLK), f32),
            jax.ShapeDtypeStruct((8, wide), jnp.int32),
            jax.ShapeDtypeStruct((full, 48, BLK), bf16),
        ),
        in_specs=[vmem()] * 8,
        out_specs=(vmem(),) * 4,
        scratch_shapes=[
            pltpu.VMEM((full, 32, BLK), f32),
            pltpu.VMEM((full, 8, BLK), f32),
            pltpu.VMEM((near.shape[1], 8), f32),
            pltpu.SMEM((8, wide), jnp.int32),
            pltpu.SemaphoreType.DMA,
        ],
        compiler_params=params(),
        name="panel_side",
    )(counts, panels, others, near, near_o, un, fe, org)


def particle_side(part, parts, pan, box, un, v, org, vn, earlier):
    build, last = vn is None, part == parts - 1
    sums = (un.shape[0], 8, BLK)
    shape = jax.ShapeDtypeStruct((3, un.shape[0] * BLK) if last else sums, f32)
    args = [pan, box, un, v, org] + ([] if build else [vn]) + list(earlier)
    return pl.pallas_call(
        functools.partial(particle_sums, part, parts, build),
        out_shape=(shape, jax.ShapeDtypeStruct(v.shape, bf16)) if build else shape,
        in_specs=[vmem()] * len(args),
        out_specs=(vmem(), vmem()) if build else vmem(),
        scratch_shapes=[pltpu.VMEM(sums, f32)] if last else [],
        compiler_params=params(),
        cost_estimate=pl.CostEstimate(flops=10**9, bytes_accessed=10**5, transcendentals=0),
        name="particle_side",
    )(*args)


def on_device(dom, panels, particles, counts, near):
    swap = [(0, 1), (1, 0)]
    others = lax.ppermute(panels, "panel", swap)
    near_o = lax.ppermute(near, "panel", swap)
    un, fe, org = prepare(particles)
    total, pan, box, v = panel_side(counts.reshape(1, -1), panels, others, near, near_o, un, fe, org)
    total = total.reshape(total.shape[1])
    steps = [1 << b for b in range((dom - 1).bit_length())]
    parts = len(steps) + 1
    chunks, factors = [], None

    for number, step in enumerate(steps):
        pairs = [(2 * i + c, 2 * (i ^ step) + 1 - c) for i in range(dom) for c in range(2)]
        total, at = lax.optimization_barrier((total, box))
        got = particle_side(number, parts, pan, at, un, v, org, factors, [])
        if factors is None:
            got, factors = got
        arrived, got = lax.optimization_barrier((lax.ppermute(total, ("dom", "panel"), pairs), got))
        chunks.append(got)
        total = total + arrived
    half = total.shape[0] // 2
    me = lax.axis_index("panel")
    total, at = lax.optimization_barrier((total, box))
    velocity = particle_side(parts - 1, parts, pan, at, un, v, org, factors, chunks)
    keep = lax.dynamic_slice(total, (me * half,), (half,))
    give = lax.dynamic_slice(total, ((1 - me) * half,), (half,))
    return keep + lax.ppermute(give, "panel", swap), velocity


def solution(mesh):
    return jax.shard_map(
        functools.partial(on_device, mesh.shape["dom"]),
        mesh=mesh,
        in_specs=(
            P(None, ("groups", "panel")),
            P(None, ("groups", "dom", "panel")),
            P(("groups", "dom", "panel")),
            P(("groups", "panel"), "dom"),
        ),
        out_specs=(P(("groups", "panel")), P(None, ("groups", "dom", "panel"))),
        check_vma=False,
    )
```

```python
import functools

import jax
import jax.numpy as jnp
from jax import lax
from jax.experimental import pallas as pl
from jax.experimental.pallas import tpu as pltpu
from jax.sharding import PartitionSpec as P

core_sq = 0.04
inv_four_pi = 0.07957747154594767
BLK = 128
WIN = 3
EACH1 = 16
EACH = 8
bf16 = jnp.bfloat16
f32 = jnp.float32


def split2(v):
    hi = v.astype(bf16)
    lo = (v - hi.astype(f32)).astype(bf16)
    return hi, lo


def split3(v):
    a = v.astype(bf16).astype(f32)
    rest = v - a
    b = rest.astype(bf16).astype(f32)
    return a, b, rest - b


def rows16(w):
    w1 = w.astype(bf16).astype(f32)
    return jnp.concatenate([w1, w - w1], axis=0).astype(bf16)


def up(v, k):
    return pltpu.roll(v, (8 - k) % 8, 0)


def rows8(width):
    return lax.broadcasted_iota(jnp.int32, (8, width), 0)


def block(q, size):
    return pl.ds(pl.multiple_of(q * size, size), size)


def particle_features(particles, un, fe, org, parts):
    nblk = particles.shape[1] // BLK
    parts[0:6, :] = particles[...]
    row = rows8(BLK)

    def one(q, carry):
        p = parts[:, block(q, BLK)]
        x = jnp.where(row < 3, p, 0.0)
        a = jnp.where(row < 3, up(p, 3), 0.0)
        xx = jnp.sum(x * x, axis=0, keepdims=True) + core_sq
        feat = jnp.where(row < 3, x, jnp.where(row < 6, 1.0, jnp.where(row == 6, xx, 0.0)))
        x1, x2, x3 = split3(feat)
        u = jnp.concatenate([x1, x1, x2, x2, x1, x3], axis=0)
        un[q] = u.astype(bf16)
        o = jnp.broadcast_to(x[:, 0:1], (8, BLK))
        d = x - o

        def rot1(v):
            return jnp.where(row < 2, up(v, 1), jnp.where(row == 2, up(v, 6), 0.0))

        def rot2(v):
            return jnp.where(row < 1, up(v, 2), jnp.where(row < 3, up(v, 7), 0.0))

        cross = rot1(d) * rot2(a) - rot2(d) * rot1(a)
        f = jnp.where(row < 3, a, up(cross, 5))
        f = jnp.where(row < 6, f, 0.0)
        f16 = rows16(f)
        fe[q] = jnp.concatenate([f16, f16], axis=1)
        for i, v in enumerate((o, rot1(o), rot2(o), d)):
            org[q, 8 * i : 8 * i + 8, :] = v
        return carry

    lax.fori_loop(0, nblk, one, 0, unroll=4)


def list_pairs(mine, other, counts, me, nblk, column, box):
    half, cols = mine.shape
    row = lax.broadcasted_iota(jnp.int32, (half, cols), 0)
    big = jnp.int32(2 * half)
    a, b = mine[...], other[...]
    first = jnp.minimum(
        jnp.min(jnp.where(a > 0, row + me * half, big), axis=0, keepdims=True),
        jnp.min(jnp.where(b > 0, row + (1 - me) * half, big), axis=0, keepdims=True),
    )
    number = jnp.sum(a, axis=0, keepdims=True) + jnp.sum(b, axis=0, keepdims=True)
    row8 = rows8(cols)
    alive = counts[...]
    if nblk < cols:
        alive = jnp.concatenate([alive, jnp.zeros((1, cols - nblk), jnp.int32)], axis=1)
    column[...] = jnp.where(row8 == 0, first, jnp.where(row8 == 1, number, alive)).astype(f32).T
    own = column[pl.ds(pl.multiple_of(me * nblk, 8), nblk), :]
    wide = box.shape[1]
    first = jnp.broadcast_to(own[:, 0:1], (nblk, wide))
    number = jnp.broadcast_to(own[:, 1:2], (nblk, wide))
    alive = jnp.broadcast_to(column[0:nblk, 2:3], (nblk, wide))
    before = lax.broadcasted_iota(jnp.int32, (nblk, nblk), 0) > lax.broadcasted_iota(jnp.int32, (nblk, nblk), 1)
    start = jnp.dot(before.astype(f32).astype(bf16), number.astype(bf16), preferred_element_type=f32)
    lane = lax.broadcasted_iota(jnp.int32, (nblk, wide), 1).astype(f32)
    block_of = lax.broadcasted_iota(jnp.int32, (nblk, wide), 0).astype(f32)
    here = (lane >= start) & (lane < start + number)
    particle = jnp.sum(jnp.where(here, block_of, 0.0), axis=0, keepdims=True)
    empty = 2.0 * half
    panel = empty + jnp.sum(jnp.where(here, first + lane - start - empty, 0.0), axis=0, keepdims=True)
    alive = jnp.sum(jnp.where(here, alive, 0.0), axis=0, keepdims=True)
    total = jnp.sum(number, axis=0, keepdims=True)
    row8 = rows8(wide)
    box[...] = jnp.where(row8 == 0, particle, jnp.where(row8 == 1, panel, jnp.where(row8 == 2, alive, total))).astype(jnp.int32)


def each_panel_block(panels, others, me, body):
    many = panels.shape[1] // BLK

    def run(ref, start):
        def one(k, carry):
            body(ref[:, block(k, BLK)], start + k)
            return carry

        lax.fori_loop(0, many, one, 0, unroll=4)

    run(panels, me * many)
    run(others, (1 - me) * many)
    for extra in range(WIN - 1):
        body(jnp.zeros((8, BLK), f32), 2 * many + extra)


def stack6(c1, c2, c3):
    pair = jnp.concatenate([c1, c2], axis=0).astype(bf16)
    return jnp.concatenate([pair, pair, jnp.concatenate([c3, c1], axis=0).astype(bf16)], axis=0)


def apart(a, b):
    none = jnp.zeros(a.shape, a.dtype)
    return jnp.concatenate([jnp.concatenate([a, none], axis=1), jnp.concatenate([none, b], axis=1)], axis=0)


TURN = (((0,), (0,)), ((), ()))


def panel_sums(counts, panels, others, near, near_o, un, fe, org, out, pan, box, v, vn, geo, tot, column, items, sem):
    me = lax.axis_index("panel")
    nblk = un.shape[0]
    list_pairs(near, near_o, counts, me, nblk, column, box)
    copy = pltpu.make_async_copy(box, items, sem)
    copy.start()
    row = rows8(BLK)

    def build(p, at):
        pan[at] = p
        c = jnp.where(row < 3, p, 0.0)
        dist = jnp.where(row < 3, -2.0 * c, jnp.where(row < 6, up(c * c, 5), jnp.where(row == 6, 1.0, 0.0)))
        v[at] = stack6(*split3(dist))
        mn3 = jnp.where(row < 3, up(p, 3) * p[7:8, :], 0.0) * 3.0
        vn[at] = stack6(*split3(jnp.where(row < 3, -mn3, up(mn3 * c, 5))))
        geo[at, 0:8, :] = jnp.where(row < 2, up(p, 4), jnp.where(row == 2, up(p, 1), jnp.where(row < 6, -p, 0.0)))
        geo[at, 8:16, :] = jnp.where(row < 1, up(p, 5), jnp.where(row < 3, up(p, 2), 0.0))
        geo[at, 16:24, :] = jnp.where(row < 2, up(p, 1), jnp.where(row == 2, up(p, 6), 0.0))
        geo[at, 24:32, :] = jnp.where(row < 1, up(p, 2), jnp.where(row < 3, up(p, 7), 1.0))
        tot[at] = jnp.zeros((8, BLK), f32)

    each_panel_block(panels, others, me, build)
    copy.wait()
    filled = items[3, 0]
    lane = lax.broadcasted_iota(jnp.int32, (16, 2 * BLK), 1) % BLK

    def moments(n):
        qa, qb = items[0, n], items[0, n + 1]
        u = jnp.concatenate([un[qa], un[qb]], axis=0)
        r2 = lax.dot_general(u, apart(v[items[1, n]], v[items[1, n + 1]]), TURN, preferred_element_type=f32)
        inv = lax.rsqrt(r2)
        hi, lo = split2(inv * inv * inv)
        f = [fe[q] * jnp.where(lane < items[2, n + i], 1.0, 0.0).astype(bf16) for i, q in enumerate((qa, qb))]
        return jnp.concatenate(f, axis=0), jnp.concatenate([hi, lo], axis=0)

    def finish(n, g):
        q, at = items[0, n], items[1, n]
        m = geo[at, 0:8, :] * (geo[at, 24:32, :] - org[q, 16:24, :]) - geo[at, 8:16, :] * (geo[at, 16:24, :] - org[q, 8:16, :])
        tot[at] += (g[0:8] + g[8:16]) * m

    def some(i, carry):
        ns = [i * EACH1 + e for e in range(0, EACH1, 2)]
        parts = [moments(n) for n in ns]
        for n, (f, k) in zip(ns, parts):
            g = jnp.dot(f, k, preferred_element_type=f32)
            finish(n, g[0:16, 0:BLK])
            finish(n + 1, g[16:32, BLK:])
        return carry

    lax.fori_loop(0, (filled + EACH1 - 1) // EACH1, some, 0)
    for k in range(out.shape[1] // BLK):
        out[:, k * BLK : (k + 1) * BLK] = -inv_four_pi * jnp.sum(tot[k], axis=0, keepdims=True)


def share(rounds, part, parts):
    return jnp.minimum(rounds, (2 * part * rounds + 2 * parts - 2) // (2 * parts - 1))


def particle_sums(part, parts, pan, items, un, v, vn, org, *rest):
    row = rows8(BLK)
    total, = rest
    total[...] = jnp.zeros(total.shape, f32)
    listed = items[...]
    filled = listed[3, 0]
    def rows(n):
        p = pan[n[1]]
        d = jnp.where(row < 3, p - org[n[0], 0:8, :], jnp.where(row == 3, 1.0, 0.0))
        mn = jnp.where(row < 3, up(p, 3) * p[7:8], 0.0)
        d16, e16 = rows16(d), rows16(-p[6:7] * d - mn)
        return jnp.concatenate([d16, d16, e16, e16], axis=1)

    def factors(n, m):
        both = [jnp.concatenate([v[at], vn[at]], axis=1) for at in (n[1], m[1])]
        u = apart(un[n[0]], un[m[0]])
        pair = lax.dot_general(jnp.concatenate(both, axis=0), u, TURN, preferred_element_type=f32)
        inv = lax.rsqrt(pair[0:BLK])
        inv2 = inv * inv
        inv3 = inv2 * inv
        t1, t2 = split2(inv3 * (inv2 * pair[BLK:]))
        i1, i2 = split2(inv3)
        return jnp.concatenate([rows(n), rows(m)], axis=0), jnp.concatenate([t1, t2, i1, i2], axis=0)

    def finish(n, h):
        q = n[0]
        h = (h[0:8] + h[8:16]) * inv_four_pi
        total[q] += h - org[q, 24:32, :] * h[3:4]

    def some(i, carry):
        now = pltpu.roll(listed, listed.shape[1] - i * EACH, 1)
        ns = [(now[0, e], now[1, e]) for e in range(EACH)]
        parts = [factors(ns[e], ns[e + 1]) for e in range(0, EACH, 2)]
        for e, (f, k) in zip(range(0, EACH, 2), parts):
            h = jnp.dot(f, k, preferred_element_type=f32)
            finish(ns[e], h[0:16, 0:BLK])
            finish(ns[e + 1], h[16:32, BLK:])
        return carry

    rounds = (filled + EACH - 1) // EACH
    lax.fori_loop(share(rounds, part, parts), share(rounds, part + 1, parts), some, 0)


def last_sums(total, arrived, *rest):
    pieces, (normal, velocity) = rest[:-2], rest[-2:]
    half = normal.shape[1]
    me = lax.axis_index("panel")
    normal[...] = total[:, pl.ds(pl.multiple_of(me * half, half), half)] + arrived[...]
    for q in range(pieces[0].shape[0]):
        velocity[:, q * BLK : (q + 1) * BLK] = sum(p[q] for p in pieces)[0:3]


def vmem():
    return pl.BlockSpec(memory_space=pltpu.VMEM)


def smem():
    return pl.BlockSpec(memory_space=pltpu.SMEM)


def params(mib=24):
    return pltpu.CompilerParams(vmem_limit_bytes=mib * 1024 * 1024)


def prepare(particles):
    width = particles.shape[1]
    nblk = width // BLK
    return pl.pallas_call(
        particle_features,
        out_shape=(
            jax.ShapeDtypeStruct((nblk, 48, BLK), bf16),
            jax.ShapeDtypeStruct((nblk, 16, 2 * BLK), bf16),
            jax.ShapeDtypeStruct((nblk, 32, BLK), f32),
        ),
        in_specs=[vmem()],
        out_specs=(vmem(),) * 3,
        scratch_shapes=[pltpu.VMEM((8, width), f32)],
        compiler_params=params(),
        cost_estimate=pl.CostEstimate(flops=2 * 10**9, bytes_accessed=10**6, transcendentals=0),
        name="prepare",
    )(particles)


def panel_side(counts, panels, others, near, near_o, un, fe, org):
    npan = 2 * panels.shape[1]
    full = npan // BLK + WIN - 1
    wide = pl.cdiv(WIN * counts.shape[1] + EACH1, BLK) * BLK
    return pl.pallas_call(
        panel_sums,
        out_shape=(
            jax.ShapeDtypeStruct((1, npan), f32),
            jax.ShapeDtypeStruct((full, 8, BLK), f32),
            jax.ShapeDtypeStruct((8, wide), jnp.int32),
            jax.ShapeDtypeStruct((full, 48, BLK), bf16),
            jax.ShapeDtypeStruct((full, 48, BLK), bf16),
        ),
        in_specs=[vmem()] * 8,
        out_specs=(vmem(),) * 5,
        scratch_shapes=[
            pltpu.VMEM((full, 32, BLK), f32),
            pltpu.VMEM((full, 8, BLK), f32),
            pltpu.VMEM((near.shape[1], 8), f32),
            pltpu.SMEM((8, wide), jnp.int32),
            pltpu.SemaphoreType.DMA,
        ],
        compiler_params=params(),
        name="panel_side",
    )(counts, panels, others, near, near_o, un, fe, org)


def particle_side(part, parts, pan, box, un, v, vn, org):
    return pl.pallas_call(
        functools.partial(particle_sums, part, parts),
        out_shape=jax.ShapeDtypeStruct((un.shape[0], 8, BLK), f32),
        in_specs=[vmem()] * 6,
        out_specs=vmem(),
        compiler_params=params(),
        cost_estimate=pl.CostEstimate(flops=10**9, bytes_accessed=10**5, transcendentals=0),
        name="particle_side",
    )(pan, box, un, v, vn, org)


def close(total, arrived, pieces):
    half = arrived.shape[0]
    normal, velocity = pl.pallas_call(
        last_sums,
        out_shape=(
            jax.ShapeDtypeStruct((1, half), f32),
            jax.ShapeDtypeStruct((3, pieces[0].shape[0] * BLK), f32),
        ),
        in_specs=[vmem()] * (2 + len(pieces)),
        out_specs=(vmem(), vmem()),
        compiler_params=params(),
        name="close",
    )(total.reshape(1, -1), arrived.reshape(1, -1), *pieces)
    return normal.reshape(half), velocity


def on_device(dom, panels, particles, counts, near):
    swap = [(0, 1), (1, 0)]
    others = lax.ppermute(panels, "panel", swap)
    near_o = lax.ppermute(near, "panel", swap)
    un, fe, org = prepare(particles)
    total, pan, box, v, vn = panel_side(counts.reshape(1, -1), panels, others, near, near_o, un, fe, org)
    total = total.reshape(total.shape[1])
    steps = [1 << b for b in range((dom - 1).bit_length())]
    parts = len(steps) + 1
    chunks = []

    for number, step in enumerate(steps):
        pairs = [(2 * i + c, 2 * (i ^ step) + 1 - c) for i in range(dom) for c in range(2)]
        total, at = lax.optimization_barrier((total, box))
        got = particle_side(number, parts, pan, at, un, v, vn, org)
        arrived, got = lax.optimization_barrier((lax.ppermute(total, ("dom", "panel"), pairs), got))
        chunks.append(got)
        total = total + arrived
    half = total.shape[0] // 2
    me = lax.axis_index("panel")
    total, at = lax.optimization_barrier((total, box))
    chunks.append(particle_side(parts - 1, parts, pan, at, un, v, vn, org))
    give = lax.dynamic_slice(total, ((1 - me) * half,), (half,))
    return close(total, lax.ppermute(give, "panel", swap), chunks)


def solution(mesh):
    return jax.shard_map(
        functools.partial(on_device, mesh.shape["dom"]),
        mesh=mesh,
        in_specs=(
            P(None, ("groups", "panel")),
            P(None, ("groups", "dom", "panel")),
            P(("groups", "dom", "panel")),
            P(("groups", "panel"), "dom"),
        ),
        out_specs=(P(("groups", "panel")), P(None, ("groups", "dom", "panel"))),
        check_vma=False,
    )
```

```python
import functools

import jax
import jax.numpy as jnp
from jax import lax
from jax.experimental import pallas as pl
from jax.experimental.pallas import tpu as pltpu
from jax.sharding import PartitionSpec as P

core_sq = 0.04
inv_four_pi = 0.07957747154594767
BLK = 128
WIN = 3
EACH1 = 20
EACH = 10
bf16 = jnp.bfloat16
f32 = jnp.float32


def split2(v):
    hi = v.astype(bf16)
    lo = (v - hi.astype(f32)).astype(bf16)
    return hi, lo


def split3(v):
    a = v.astype(bf16).astype(f32)
    rest = v - a
    b = rest.astype(bf16).astype(f32)
    return a, b, rest - b


def rows16(w):
    w1 = w.astype(bf16).astype(f32)
    return jnp.concatenate([w1, w - w1], axis=0).astype(bf16)


def up(v, k):
    return pltpu.roll(v, (8 - k) % 8, 0)


def rows8(width):
    return lax.broadcasted_iota(jnp.int32, (8, width), 0)


def block(q, size):
    return pl.ds(pl.multiple_of(q * size, size), size)


def particle_features(particles, un, fe, org, parts):
    nblk = particles.shape[1] // BLK
    parts[0:6, :] = particles[...]
    row = rows8(BLK)

    def one(q, carry):
        p = parts[:, block(q, BLK)]
        x = jnp.where(row < 3, p, 0.0)
        a = jnp.where(row < 3, up(p, 3), 0.0)
        xx = jnp.sum(x * x, axis=0, keepdims=True) + core_sq
        feat = jnp.where(row < 3, x, jnp.where(row < 6, 1.0, jnp.where(row == 6, xx, 0.0)))
        x1, x2, x3 = split3(feat)
        u = jnp.concatenate([x1, x1, x2, x2, x1, x3], axis=0)
        un[q] = u.astype(bf16)
        o = jnp.broadcast_to(x[:, 0:1], (8, BLK))
        d = x - o

        def rot1(v):
            return jnp.where(row < 2, up(v, 1), jnp.where(row == 2, up(v, 6), 0.0))

        def rot2(v):
            return jnp.where(row < 1, up(v, 2), jnp.where(row < 3, up(v, 7), 0.0))

        cross = rot1(d) * rot2(a) - rot2(d) * rot1(a)
        f = jnp.where(row < 3, a, up(cross, 5))
        f = jnp.where(row < 6, f, 0.0)
        f16 = rows16(f)
        fe[q] = jnp.concatenate([f16, f16], axis=1)
        for i, v in enumerate((o, rot1(o), rot2(o), d)):
            org[q, 8 * i : 8 * i + 8, :] = v
        return carry

    lax.fori_loop(0, nblk, one, 0, unroll=4)


def list_pairs(mine, other, counts, me, nblk, column, box):
    half, cols = mine.shape
    row = lax.broadcasted_iota(jnp.int32, (half, cols), 0)
    big = jnp.int32(2 * half)
    a, b = mine[...], other[...]
    first = jnp.minimum(
        jnp.min(jnp.where(a > 0, row + me * half, big), axis=0, keepdims=True),
        jnp.min(jnp.where(b > 0, row + (1 - me) * half, big), axis=0, keepdims=True),
    )
    number = jnp.sum(a, axis=0, keepdims=True) + jnp.sum(b, axis=0, keepdims=True)
    row8 = rows8(cols)
    alive = counts[...]
    if nblk < cols:
        alive = jnp.concatenate([alive, jnp.zeros((1, cols - nblk), jnp.int32)], axis=1)
    column[...] = jnp.where(row8 == 0, first, jnp.where(row8 == 1, number, alive)).astype(f32).T
    own = column[pl.ds(pl.multiple_of(me * nblk, 8), nblk), :]
    wide = box.shape[1]
    first = jnp.broadcast_to(own[:, 0:1], (nblk, wide))
    number = jnp.broadcast_to(own[:, 1:2], (nblk, wide))
    alive = jnp.broadcast_to(column[0:nblk, 2:3], (nblk, wide))
    before = lax.broadcasted_iota(jnp.int32, (nblk, nblk), 0) > lax.broadcasted_iota(jnp.int32, (nblk, nblk), 1)
    start = jnp.dot(before.astype(f32).astype(bf16), number.astype(bf16), preferred_element_type=f32)
    lane = lax.broadcasted_iota(jnp.int32, (nblk, wide), 1).astype(f32)
    block_of = lax.broadcasted_iota(jnp.int32, (nblk, wide), 0).astype(f32)
    here = (lane >= start) & (lane < start + number)
    particle = jnp.sum(jnp.where(here, block_of, 0.0), axis=0, keepdims=True)
    empty = 2.0 * half
    panel = empty + jnp.sum(jnp.where(here, first + lane - start - empty, 0.0), axis=0, keepdims=True)
    alive = jnp.sum(jnp.where(here, alive, 0.0), axis=0, keepdims=True)
    total = jnp.sum(number, axis=0, keepdims=True)
    row8 = rows8(wide)
    box[...] = jnp.where(row8 == 0, particle, jnp.where(row8 == 1, panel, jnp.where(row8 == 2, alive, total))).astype(jnp.int32)


def each_panel_block(panels, others, me, body):
    many = panels.shape[1] // BLK

    def run(ref, start):
        def one(k, carry):
            body(ref[:, block(k, BLK)], start + k)
            return carry

        lax.fori_loop(0, many, one, 0, unroll=4)

    run(panels, me * many)
    run(others, (1 - me) * many)
    for extra in range(WIN - 1):
        body(jnp.zeros((8, BLK), f32), 2 * many + extra)


def stack6(c1, c2, c3):
    pair = jnp.concatenate([c1, c2], axis=0).astype(bf16)
    return jnp.concatenate([pair, pair, jnp.concatenate([c3, c1], axis=0).astype(bf16)], axis=0)


def apart(a, b):
    none = jnp.zeros(a.shape, a.dtype)
    return jnp.concatenate([jnp.concatenate([a, none], axis=1), jnp.concatenate([none, b], axis=1)], axis=0)


TURN = (((0,), (0,)), ((), ()))


def panel_sums(counts, panels, others, near, near_o, un, fe, org, out, pan, box, v, vn, geo, tot, column, items, sem):
    me = lax.axis_index("panel")
    nblk = un.shape[0]
    list_pairs(near, near_o, counts, me, nblk, column, box)
    copy = pltpu.make_async_copy(box, items, sem)
    copy.start()
    row = rows8(BLK)

    def build(p, at):
        pan[at] = p
        c = jnp.where(row < 3, p, 0.0)
        dist = jnp.where(row < 3, -2.0 * c, jnp.where(row < 6, up(c * c, 5), jnp.where(row == 6, 1.0, 0.0)))
        v[at] = stack6(*split3(dist))
        mn3 = jnp.where(row < 3, up(p, 3) * p[7:8, :], 0.0) * 3.0
        vn[at] = stack6(*split3(jnp.where(row < 3, -mn3, up(mn3 * c, 5))))
        geo[at, 0:8, :] = jnp.where(row < 2, up(p, 4), jnp.where(row == 2, up(p, 1), jnp.where(row < 6, -p, 0.0)))
        geo[at, 8:16, :] = jnp.where(row < 1, up(p, 5), jnp.where(row < 3, up(p, 2), 0.0))
        geo[at, 16:24, :] = jnp.where(row < 2, up(p, 1), jnp.where(row == 2, up(p, 6), 0.0))
        geo[at, 24:32, :] = jnp.where(row < 1, up(p, 2), jnp.where(row < 3, up(p, 7), 1.0))
        tot[at] = jnp.zeros((8, BLK), f32)

    each_panel_block(panels, others, me, build)
    copy.wait()
    filled = items[3, 0]
    lane = lax.broadcasted_iota(jnp.int32, (16, 2 * BLK), 1) % BLK

    def moments(n):
        qa, qb = items[0, n], items[0, n + 1]
        u = jnp.concatenate([un[qa], un[qb]], axis=0)
        r2 = lax.dot_general(u, apart(v[items[1, n]], v[items[1, n + 1]]), TURN, preferred_element_type=f32)
        inv = lax.rsqrt(r2)
        hi, lo = split2(inv * inv * inv)
        f = [fe[q] * jnp.where(lane < items[2, n + i], 1.0, 0.0).astype(bf16) for i, q in enumerate((qa, qb))]
        return jnp.concatenate(f, axis=0), jnp.concatenate([hi, lo], axis=0)

    def finish(n, g):
        q, at = items[0, n], items[1, n]
        m = geo[at, 0:8, :] * (geo[at, 24:32, :] - org[q, 16:24, :]) - geo[at, 8:16, :] * (geo[at, 16:24, :] - org[q, 8:16, :])
        tot[at] += (g[0:8] + g[8:16]) * m

    def some(i, carry):
        ns = [i * EACH1 + e for e in range(0, EACH1, 2)]
        parts = [moments(n) for n in ns]
        for n, (f, k) in zip(ns, parts):
            g = jnp.dot(f, k, preferred_element_type=f32)
            finish(n, g[0:16, 0:BLK])
            finish(n + 1, g[16:32, BLK:])
        return carry

    lax.fori_loop(0, (filled + EACH1 - 1) // EACH1, some, 0)
    for k in range(out.shape[1] // BLK):
        out[:, k * BLK : (k + 1) * BLK] = -inv_four_pi * jnp.sum(tot[k], axis=0, keepdims=True)


def share(rounds, part, parts):
    return jnp.minimum(rounds, (part * rounds + parts - 1) // parts)


def particle_sums(part, parts, pan, items, un, v, vn, org, *rest):
    row = rows8(BLK)
    total, = rest
    total[...] = jnp.zeros(total.shape, f32)
    listed = items[...]
    filled = listed[3, 0]
    def rows(n):
        p = pan[n[1]]
        d = jnp.where(row < 3, p - org[n[0], 0:8, :], jnp.where(row == 3, 1.0, 0.0))
        mn = jnp.where(row < 3, up(p, 3) * p[7:8], 0.0)
        d16, e16 = rows16(d), rows16(-p[6:7] * d - mn)
        return jnp.concatenate([d16, d16, e16, e16], axis=1)

    def factors(n, m):
        both = [jnp.concatenate([v[at], vn[at]], axis=1) for at in (n[1], m[1])]
        u = apart(un[n[0]], un[m[0]])
        pair = lax.dot_general(jnp.concatenate(both, axis=0), u, TURN, preferred_element_type=f32)
        inv = lax.rsqrt(pair[0:BLK])
        inv2 = inv * inv
        inv3 = inv2 * inv
        t1, t2 = split2(inv3 * (inv2 * pair[BLK:]))
        i1, i2 = split2(inv3)
        return jnp.concatenate([rows(n), rows(m)], axis=0), jnp.concatenate([t1, t2, i1, i2], axis=0)

    def finish(n, h):
        q = n[0]
        h = (h[0:8] + h[8:16]) * inv_four_pi
        total[q] += h - org[q, 24:32, :] * h[3:4]

    def some(i, carry):
        now = pltpu.roll(listed, listed.shape[1] - i * EACH, 1)
        ns = [(now[0, e], now[1, e]) for e in range(EACH)]
        parts = [factors(ns[e], ns[e + 1]) for e in range(0, EACH, 2)]
        for e, (f, k) in zip(range(0, EACH, 2), parts):
            h = jnp.dot(f, k, preferred_element_type=f32)
            finish(ns[e], h[0:16, 0:BLK])
            finish(ns[e + 1], h[16:32, BLK:])
        return carry

    rounds = (filled + EACH - 1) // EACH
    lax.fori_loop(share(rounds, part, parts), share(rounds, part + 1, parts), some, 0)


def last_sums(total, arrived, *rest):
    pieces, (normal, velocity) = rest[:-2], rest[-2:]
    half = normal.shape[1]
    me = lax.axis_index("panel")
    normal[...] = total[:, pl.ds(pl.multiple_of(me * half, half), half)] + arrived[...]
    for q in range(pieces[0].shape[0]):
        velocity[:, q * BLK : (q + 1) * BLK] = sum(p[q] for p in pieces)[0:3]


def vmem():
    return pl.BlockSpec(memory_space=pltpu.VMEM)


def smem():
    return pl.BlockSpec(memory_space=pltpu.SMEM)


def params(mib=24):
    return pltpu.CompilerParams(vmem_limit_bytes=mib * 1024 * 1024)


def prepare(particles):
    width = particles.shape[1]
    nblk = width // BLK
    return pl.pallas_call(
        particle_features,
        out_shape=(
            jax.ShapeDtypeStruct((nblk, 48, BLK), bf16),
            jax.ShapeDtypeStruct((nblk, 16, 2 * BLK), bf16),
            jax.ShapeDtypeStruct((nblk, 32, BLK), f32),
        ),
        in_specs=[vmem()],
        out_specs=(vmem(),) * 3,
        scratch_shapes=[pltpu.VMEM((8, width), f32)],
        compiler_params=params(),
        cost_estimate=pl.CostEstimate(flops=2 * 10**9, bytes_accessed=10**6, transcendentals=0),
        name="prepare",
    )(particles)


def panel_side(counts, panels, others, near, near_o, un, fe, org):
    npan = 2 * panels.shape[1]
    full = npan // BLK + WIN - 1
    wide = pl.cdiv(WIN * counts.shape[1] + EACH1, BLK) * BLK
    return pl.pallas_call(
        panel_sums,
        out_shape=(
            jax.ShapeDtypeStruct((1, npan), f32),
            jax.ShapeDtypeStruct((full, 8, BLK), f32),
            jax.ShapeDtypeStruct((8, wide), jnp.int32),
            jax.ShapeDtypeStruct((full, 48, BLK), bf16),
            jax.ShapeDtypeStruct((full, 48, BLK), bf16),
        ),
        in_specs=[vmem()] * 8,
        out_specs=(vmem(),) * 5,
        scratch_shapes=[
            pltpu.VMEM((full, 32, BLK), f32),
            pltpu.VMEM((full, 8, BLK), f32),
            pltpu.VMEM((near.shape[1], 8), f32),
            pltpu.SMEM((8, wide), jnp.int32),
            pltpu.SemaphoreType.DMA,
        ],
        compiler_params=params(),
        name="panel_side",
    )(counts, panels, others, near, near_o, un, fe, org)


def particle_side(part, parts, pan, box, un, v, vn, org):
    return pl.pallas_call(
        functools.partial(particle_sums, part, parts),
        out_shape=jax.ShapeDtypeStruct((un.shape[0], 8, BLK), f32),
        in_specs=[vmem()] * 6,
        out_specs=vmem(),
        compiler_params=params(),
        cost_estimate=pl.CostEstimate(flops=10**9, bytes_accessed=10**5, transcendentals=0),
        name="particle_side",
    )(pan, box, un, v, vn, org)


def close(total, arrived, pieces):
    half = arrived.shape[0]
    normal, velocity = pl.pallas_call(
        last_sums,
        out_shape=(
            jax.ShapeDtypeStruct((1, half), f32),
            jax.ShapeDtypeStruct((3, pieces[0].shape[0] * BLK), f32),
        ),
        in_specs=[vmem()] * (2 + len(pieces)),
        out_specs=(vmem(), vmem()),
        compiler_params=params(),
        name="close",
    )(total.reshape(1, -1), arrived.reshape(1, -1), *pieces)
    return normal.reshape(half), velocity


def on_device(dom, panels, particles, counts, near):
    swap = [(0, 1), (1, 0)]
    others = lax.ppermute(panels, "panel", swap)
    near_o = lax.ppermute(near, "panel", swap)
    un, fe, org = prepare(particles)
    total, pan, box, v, vn = panel_side(counts.reshape(1, -1), panels, others, near, near_o, un, fe, org)
    total = total.reshape(total.shape[1])
    steps = [1 << b for b in range((dom - 1).bit_length())]
    parts = len(steps) + 1
    chunks = []

    for number, step in enumerate(steps):
        pairs = [(2 * i + c, 2 * (i ^ step) + 1 - c) for i in range(dom) for c in range(2)]
        total, at = lax.optimization_barrier((total, box))
        got = particle_side(number, parts, pan, at, un, v, vn, org)
        arrived, got = lax.optimization_barrier((lax.ppermute(total, ("dom", "panel"), pairs), got))
        chunks.append(got)
        total = total + arrived
    half = total.shape[0] // 2
    me = lax.axis_index("panel")
    total, at = lax.optimization_barrier((total, box))
    chunks.append(particle_side(parts - 1, parts, pan, at, un, v, vn, org))
    give = lax.dynamic_slice(total, ((1 - me) * half,), (half,))
    return close(total, lax.ppermute(give, "panel", swap), chunks)


def solution(mesh):
    return jax.shard_map(
        functools.partial(on_device, mesh.shape["dom"]),
        mesh=mesh,
        in_specs=(
            P(None, ("groups", "panel")),
            P(None, ("groups", "dom", "panel")),
            P(("groups", "dom", "panel")),
            P(("groups", "panel"), "dom"),
        ),
        out_specs=(P(("groups", "panel")), P(None, ("groups", "dom", "panel"))),
        check_vma=False,
    )
```

```python
import functools

import jax
import jax.numpy as jnp
from jax import lax
from jax.experimental import pallas as pl
from jax.experimental.pallas import tpu as pltpu
from jax.sharding import PartitionSpec as P

core_sq = 0.04
inv_four_pi = 0.07957747154594767
BLK = 128
WIN = 3
EACH1 = 26
EACH = 10
bf16 = jnp.bfloat16
f32 = jnp.float32


def split2(v):
    hi = v.astype(bf16)
    lo = (v - hi.astype(f32)).astype(bf16)
    return hi, lo


def split3(v):
    a = v.astype(bf16).astype(f32)
    rest = v - a
    b = rest.astype(bf16).astype(f32)
    return a, b, rest - b


def rows16(w):
    w1 = w.astype(bf16).astype(f32)
    return jnp.concatenate([w1, w - w1], axis=0).astype(bf16)


def up(v, k):
    return pltpu.roll(v, (8 - k) % 8, 0)


def rows8(width):
    return lax.broadcasted_iota(jnp.int32, (8, width), 0)


def block(q, size):
    return pl.ds(pl.multiple_of(q * size, size), size)


def particle_features(particles, un, fe, org, parts):
    nblk = particles.shape[1] // BLK
    parts[0:6, :] = particles[...]
    row = rows8(BLK)

    def one(q, carry):
        p = parts[:, block(q, BLK)]
        x = jnp.where(row < 3, p, 0.0)
        a = jnp.where(row < 3, up(p, 3), 0.0)
        xx = jnp.sum(x * x, axis=0, keepdims=True) + core_sq
        feat = jnp.where(row < 3, x, jnp.where(row < 6, 1.0, jnp.where(row == 6, xx, 0.0)))
        x1, x2, x3 = split3(feat)
        u = jnp.concatenate([x1, x1, x2, x2, x1, x3], axis=0)
        un[q] = u.astype(bf16)
        o = jnp.broadcast_to(x[:, 0:1], (8, BLK))
        d = x - o

        def rot1(v):
            return jnp.where(row < 2, up(v, 1), jnp.where(row == 2, up(v, 6), 0.0))

        def rot2(v):
            return jnp.where(row < 1, up(v, 2), jnp.where(row < 3, up(v, 7), 0.0))

        cross = rot1(d) * rot2(a) - rot2(d) * rot1(a)
        f = jnp.where(row < 3, a, up(cross, 5))
        f = jnp.where(row < 6, f, 0.0)
        f16 = rows16(f)
        fe[q] = jnp.concatenate([f16, f16], axis=1)
        for i, v in enumerate((o, rot1(o), rot2(o), d)):
            org[q, 8 * i : 8 * i + 8, :] = v
        return carry

    lax.fori_loop(0, nblk, one, 0, unroll=16)


def list_pairs(mine, other, counts, me, nblk, column, box):
    half, cols = mine.shape
    row = lax.broadcasted_iota(jnp.int32, (half, cols), 0)
    big = jnp.int32(2 * half)
    a, b = mine[...], other[...]
    first = jnp.minimum(
        jnp.min(jnp.where(a > 0, row + me * half, big), axis=0, keepdims=True),
        jnp.min(jnp.where(b > 0, row + (1 - me) * half, big), axis=0, keepdims=True),
    )
    number = jnp.sum(a, axis=0, keepdims=True) + jnp.sum(b, axis=0, keepdims=True)
    row8 = rows8(cols)
    alive = counts[...]
    if nblk < cols:
        alive = jnp.concatenate([alive, jnp.zeros((1, cols - nblk), jnp.int32)], axis=1)
    column[...] = jnp.where(row8 == 0, first, jnp.where(row8 == 1, number, alive)).astype(f32).T
    own = column[pl.ds(pl.multiple_of(me * nblk, 8), nblk), :]
    wide = box.shape[1]
    first = jnp.broadcast_to(own[:, 0:1], (nblk, wide))
    number = jnp.broadcast_to(own[:, 1:2], (nblk, wide))
    alive = jnp.broadcast_to(column[0:nblk, 2:3], (nblk, wide))
    before = lax.broadcasted_iota(jnp.int32, (nblk, nblk), 0) > lax.broadcasted_iota(jnp.int32, (nblk, nblk), 1)
    start = jnp.dot(before.astype(f32).astype(bf16), number.astype(bf16), preferred_element_type=f32)
    lane = lax.broadcasted_iota(jnp.int32, (nblk, wide), 1).astype(f32)
    block_of = lax.broadcasted_iota(jnp.int32, (nblk, wide), 0).astype(f32)
    here = (lane >= start) & (lane < start + number)
    particle = jnp.sum(jnp.where(here, block_of, 0.0), axis=0, keepdims=True)
    empty = 2.0 * half
    panel = empty + jnp.sum(jnp.where(here, first + lane - start - empty, 0.0), axis=0, keepdims=True)
    alive = jnp.sum(jnp.where(here, alive, 0.0), axis=0, keepdims=True)
    total = jnp.sum(number, axis=0, keepdims=True)
    row8 = rows8(wide)
    box[...] = jnp.where(row8 == 0, particle, jnp.where(row8 == 1, panel, jnp.where(row8 == 2, alive, total))).astype(jnp.int32)


def each_panel_block(panels, others, me, body):
    many = panels.shape[1] // BLK

    def run(ref, start):
        def one(k, carry):
            body(ref[:, block(k, BLK)], start + k)
            return carry

        lax.fori_loop(0, many, one, 0, unroll=8)

    run(panels, me * many)
    run(others, (1 - me) * many)
    for extra in range(WIN - 1):
        body(jnp.zeros((8, BLK), f32), 2 * many + extra)


def stack6(c1, c2, c3):
    pair = jnp.concatenate([c1, c2], axis=0).astype(bf16)
    return jnp.concatenate([pair, pair, jnp.concatenate([c3, c1], axis=0).astype(bf16)], axis=0)


def apart(a, b):
    none = jnp.zeros(a.shape, a.dtype)
    return jnp.concatenate([jnp.concatenate([a, none], axis=1), jnp.concatenate([none, b], axis=1)], axis=0)


TURN = (((0,), (0,)), ((), ()))


def panel_sums(counts, panels, others, near, near_o, un, fe, org, out, pan, box, v, vn, geo, tot, column, items, sem):
    me = lax.axis_index("panel")
    nblk = un.shape[0]
    list_pairs(near, near_o, counts, me, nblk, column, box)
    copy = pltpu.make_async_copy(box, items, sem)
    copy.start()
    row = rows8(BLK)

    def build(p, at):
        pan[at] = p
        c = jnp.where(row < 3, p, 0.0)
        dist = jnp.where(row < 3, -2.0 * c, jnp.where(row < 6, up(c * c, 5), jnp.where(row == 6, 1.0, 0.0)))
        v[at] = stack6(*split3(dist))
        mn3 = jnp.where(row < 3, up(p, 3) * p[7:8, :], 0.0) * 3.0
        vn[at] = stack6(*split3(jnp.where(row < 3, -mn3, up(mn3 * c, 5))))
        geo[at, 0:8, :] = jnp.where(row < 2, up(p, 4), jnp.where(row == 2, up(p, 1), jnp.where(row < 6, -p, 0.0)))
        geo[at, 8:16, :] = jnp.where(row < 1, up(p, 5), jnp.where(row < 3, up(p, 2), 0.0))
        geo[at, 16:24, :] = jnp.where(row < 2, up(p, 1), jnp.where(row == 2, up(p, 6), 0.0))
        geo[at, 24:32, :] = jnp.where(row < 1, up(p, 2), jnp.where(row < 3, up(p, 7), 1.0))
        tot[at] = jnp.zeros((8, BLK), f32)

    each_panel_block(panels, others, me, build)
    copy.wait()
    filled = items[3, 0]
    lane = lax.broadcasted_iota(jnp.int32, (16, 2 * BLK), 1) % BLK

    def moments(n):
        qa, qb = items[0, n], items[0, n + 1]
        u = jnp.concatenate([un[qa], un[qb]], axis=0)
        r2 = lax.dot_general(u, apart(v[items[1, n]], v[items[1, n + 1]]), TURN, preferred_element_type=f32)
        inv = lax.rsqrt(r2)
        hi, lo = split2(inv * inv * inv)
        f = [fe[q] * jnp.where(lane < items[2, n + i], 1.0, 0.0).astype(bf16) for i, q in enumerate((qa, qb))]
        return jnp.concatenate(f, axis=0), jnp.concatenate([hi, lo], axis=0)

    def finish(n, g):
        q, at = items[0, n], items[1, n]
        m = geo[at, 0:8, :] * (geo[at, 24:32, :] - org[q, 16:24, :]) - geo[at, 8:16, :] * (geo[at, 16:24, :] - org[q, 8:16, :])
        tot[at] += (g[0:8] + g[8:16]) * m

    def some(i, carry):
        ns = [i * EACH1 + e for e in range(0, EACH1, 2)]
        parts = [moments(n) for n in ns]
        for n, (f, k) in zip(ns, parts):
            g = jnp.dot(f, k, preferred_element_type=f32)
            finish(n, g[0:16, 0:BLK])
            finish(n + 1, g[16:32, BLK:])
        return carry

    lax.fori_loop(0, (filled + EACH1 - 1) // EACH1, some, 0)
    for k in range(out.shape[1] // BLK):
        out[:, k * BLK : (k + 1) * BLK] = -inv_four_pi * jnp.sum(tot[k], axis=0, keepdims=True)


def share(rounds, part, parts):
    return jnp.minimum(rounds, (part * rounds + parts - 1) // parts)


def particle_sums(part, parts, pan, items, un, v, vn, org, *rest):
    row = rows8(BLK)
    total, = rest
    total[...] = jnp.zeros(total.shape, f32)
    listed = items[...]
    filled = listed[3, 0]
    def rows(n):
        p = pan[n[1]]
        d = jnp.where(row < 3, p - org[n[0], 0:8, :], jnp.where(row == 3, 1.0, 0.0))
        mn = jnp.where(row < 3, up(p, 3) * p[7:8], 0.0)
        d16, e16 = rows16(d), rows16(-p[6:7] * d - mn)
        return jnp.concatenate([d16, d16, e16, e16], axis=1)

    def factors(n, m):
        both = [jnp.concatenate([v[at], vn[at]], axis=1) for at in (n[1], m[1])]
        u = apart(un[n[0]], un[m[0]])
        pair = lax.dot_general(jnp.concatenate(both, axis=0), u, TURN, preferred_element_type=f32)
        inv = lax.rsqrt(pair[0:BLK])
        inv2 = inv * inv
        inv3 = inv2 * inv
        t1, t2 = split2(inv3 * (inv2 * pair[BLK:]))
        i1, i2 = split2(inv3)
        return jnp.concatenate([rows(n), rows(m)], axis=0), jnp.concatenate([t1, t2, i1, i2], axis=0)

    def finish(n, h):
        q = n[0]
        h = (h[0:8] + h[8:16]) * inv_four_pi
        total[q] += h - org[q, 24:32, :] * h[3:4]

    def some(i, carry):
        now = pltpu.roll(listed, listed.shape[1] - i * EACH, 1)
        ns = [(now[0, e], now[1, e]) for e in range(EACH)]
        parts = [factors(ns[e], ns[e + 1]) for e in range(0, EACH, 2)]
        for e, (f, k) in zip(range(0, EACH, 2), parts):
            h = jnp.dot(f, k, preferred_element_type=f32)
            finish(ns[e], h[0:16, 0:BLK])
            finish(ns[e + 1], h[16:32, BLK:])
        return carry

    rounds = (filled + EACH - 1) // EACH
    lax.fori_loop(share(rounds, part, parts), share(rounds, part + 1, parts), some, 0)


def last_sums(total, arrived, *rest):
    pieces, (normal, velocity) = rest[:-2], rest[-2:]
    half = normal.shape[1]
    me = lax.axis_index("panel")
    normal[...] = total[:, pl.ds(pl.multiple_of(me * half, half), half)] + arrived[...]
    for q in range(pieces[0].shape[0]):
        velocity[:, q * BLK : (q + 1) * BLK] = sum(p[q] for p in pieces)[0:3]


def vmem():
    return pl.BlockSpec(memory_space=pltpu.VMEM)


def smem():
    return pl.BlockSpec(memory_space=pltpu.SMEM)


def params(mib=24):
    return pltpu.CompilerParams(vmem_limit_bytes=mib * 1024 * 1024)


def prepare(particles):
    width = particles.shape[1]
    nblk = width // BLK
    return pl.pallas_call(
        particle_features,
        out_shape=(
            jax.ShapeDtypeStruct((nblk, 48, BLK), bf16),
            jax.ShapeDtypeStruct((nblk, 16, 2 * BLK), bf16),
            jax.ShapeDtypeStruct((nblk, 32, BLK), f32),
        ),
        in_specs=[vmem()],
        out_specs=(vmem(),) * 3,
        scratch_shapes=[pltpu.VMEM((8, width), f32)],
        compiler_params=params(),
        cost_estimate=pl.CostEstimate(flops=2 * 10**9, bytes_accessed=10**6, transcendentals=0),
        name="prepare",
    )(particles)


def panel_side(counts, panels, others, near, near_o, un, fe, org):
    npan = 2 * panels.shape[1]
    full = npan // BLK + WIN - 1
    wide = pl.cdiv(WIN * counts.shape[1] + EACH1, BLK) * BLK
    return pl.pallas_call(
        panel_sums,
        out_shape=(
            jax.ShapeDtypeStruct((1, npan), f32),
            jax.ShapeDtypeStruct((full, 8, BLK), f32),
            jax.ShapeDtypeStruct((8, wide), jnp.int32),
            jax.ShapeDtypeStruct((full, 48, BLK), bf16),
            jax.ShapeDtypeStruct((full, 48, BLK), bf16),
        ),
        in_specs=[vmem()] * 8,
        out_specs=(vmem(),) * 5,
        scratch_shapes=[
            pltpu.VMEM((full, 32, BLK), f32),
            pltpu.VMEM((full, 8, BLK), f32),
            pltpu.VMEM((near.shape[1], 8), f32),
            pltpu.SMEM((8, wide), jnp.int32),
            pltpu.SemaphoreType.DMA,
        ],
        compiler_params=params(),
        name="panel_side",
    )(counts, panels, others, near, near_o, un, fe, org)


def particle_side(part, parts, pan, box, un, v, vn, org):
    return pl.pallas_call(
        functools.partial(particle_sums, part, parts),
        out_shape=jax.ShapeDtypeStruct((un.shape[0], 8, BLK), f32),
        in_specs=[vmem()] * 6,
        out_specs=vmem(),
        compiler_params=params(),
        cost_estimate=pl.CostEstimate(flops=10**9, bytes_accessed=10**5, transcendentals=0),
        name="particle_side",
    )(pan, box, un, v, vn, org)


def close(total, arrived, pieces):
    half = arrived.shape[0]
    normal, velocity = pl.pallas_call(
        last_sums,
        out_shape=(
            jax.ShapeDtypeStruct((1, half), f32),
            jax.ShapeDtypeStruct((3, pieces[0].shape[0] * BLK), f32),
        ),
        in_specs=[vmem()] * (2 + len(pieces)),
        out_specs=(vmem(), vmem()),
        compiler_params=params(),
        name="close",
    )(total.reshape(1, -1), arrived.reshape(1, -1), *pieces)
    return normal.reshape(half), velocity


def on_device(dom, panels, particles, counts, near):
    swap = [(0, 1), (1, 0)]
    others = lax.ppermute(panels, "panel", swap)
    near_o = lax.ppermute(near, "panel", swap)
    un, fe, org = prepare(particles)
    total, pan, box, v, vn = panel_side(counts.reshape(1, -1), panels, others, near, near_o, un, fe, org)
    total = total.reshape(total.shape[1])
    steps = [1 << b for b in range((dom - 1).bit_length())]
    parts = len(steps) + 1
    chunks = []

    for number, step in enumerate(steps):
        pairs = [(2 * i + c, 2 * (i ^ step) + 1 - c) for i in range(dom) for c in range(2)]
        total, at = lax.optimization_barrier((total, box))
        got = particle_side(number, parts, pan, at, un, v, vn, org)
        arrived, got = lax.optimization_barrier((lax.ppermute(total, ("dom", "panel"), pairs), got))
        chunks.append(got)
        total = total + arrived
    half = total.shape[0] // 2
    me = lax.axis_index("panel")
    total, at = lax.optimization_barrier((total, box))
    chunks.append(particle_side(parts - 1, parts, pan, at, un, v, vn, org))
    give = lax.dynamic_slice(total, ((1 - me) * half,), (half,))
    return close(total, lax.ppermute(give, "panel", swap), chunks)


def solution(mesh):
    return jax.shard_map(
        functools.partial(on_device, mesh.shape["dom"]),
        mesh=mesh,
        in_specs=(
            P(None, ("groups", "panel")),
            P(None, ("groups", "dom", "panel")),
            P(("groups", "dom", "panel")),
            P(("groups", "panel"), "dom"),
        ),
        out_specs=(P(("groups", "panel")), P(None, ("groups", "dom", "panel"))),
        check_vma=False,
    )
```

```python
import functools

import jax
import jax.numpy as jnp
from jax import lax
from jax.experimental import pallas as pl
from jax.experimental.pallas import tpu as pltpu
from jax.sharding import PartitionSpec as P

core_sq = 0.04
inv_four_pi = 0.07957747154594767
BLK = 128
WIN = 3
EACH1 = 26
EACH = 10
bf16 = jnp.bfloat16
f32 = jnp.float32


def split2(v):
    hi = v.astype(bf16)
    lo = (v - hi.astype(f32)).astype(bf16)
    return hi, lo


def split3(v):
    a = v.astype(bf16).astype(f32)
    rest = v - a
    b = rest.astype(bf16).astype(f32)
    return a, b, rest - b


def rows16(w):
    w1 = w.astype(bf16).astype(f32)
    return jnp.concatenate([w1, w - w1], axis=0).astype(bf16)


def up(v, k):
    return pltpu.roll(v, (8 - k) % 8, 0)


def rows8(width):
    return lax.broadcasted_iota(jnp.int32, (8, width), 0)


def block(q, size):
    return pl.ds(pl.multiple_of(q * size, size), size)


def particle_features(parts, un, fe, org):
    nblk = parts.shape[1] // BLK
    row = rows8(BLK)

    def one(q, carry):
        p = parts[:, block(q, BLK)]
        x = jnp.where(row < 3, p, 0.0)
        a = jnp.where(row < 3, up(p, 3), 0.0)
        xx = jnp.sum(x * x, axis=0, keepdims=True) + core_sq
        feat = jnp.where(row < 3, x, jnp.where(row < 6, 1.0, jnp.where(row == 6, xx, 0.0)))
        x1, x2, x3 = split3(feat)
        u = jnp.concatenate([x1, x1, x2, x2, x1, x3], axis=0)
        un[q] = u.astype(bf16)
        o = jnp.broadcast_to(x[:, 0:1], (8, BLK))
        d = x - o

        def rot1(v):
            return jnp.where(row < 2, up(v, 1), jnp.where(row == 2, up(v, 6), 0.0))

        def rot2(v):
            return jnp.where(row < 1, up(v, 2), jnp.where(row < 3, up(v, 7), 0.0))

        cross = rot1(d) * rot2(a) - rot2(d) * rot1(a)
        f = jnp.where(row < 3, a, up(cross, 5))
        f = jnp.where(row < 6, f, 0.0)
        f16 = rows16(f)
        fe[q] = jnp.concatenate([f16, f16], axis=1)
        for i, v in enumerate((o, rot1(o), rot2(o), d)):
            org[q, 8 * i : 8 * i + 8, :] = v
        return carry

    lax.fori_loop(0, nblk, one, 0, unroll=16)


def list_pairs(mine, other, counts, me, nblk, column, box):
    half, cols = mine.shape
    row = lax.broadcasted_iota(jnp.int32, (half, cols), 0)
    big = jnp.int32(2 * half)
    a, b = mine[...], other[...]
    first = jnp.minimum(
        jnp.min(jnp.where(a > 0, row + me * half, big), axis=0, keepdims=True),
        jnp.min(jnp.where(b > 0, row + (1 - me) * half, big), axis=0, keepdims=True),
    )
    number = jnp.sum(a, axis=0, keepdims=True) + jnp.sum(b, axis=0, keepdims=True)
    row8 = rows8(cols)
    alive = counts[...]
    if nblk < cols:
        alive = jnp.concatenate([alive, jnp.zeros((1, cols - nblk), jnp.int32)], axis=1)
    column[...] = jnp.where(row8 == 0, first, jnp.where(row8 == 1, number, alive)).astype(f32).T
    own = column[pl.ds(pl.multiple_of(me * nblk, 8), nblk), :]
    wide = box.shape[1]
    first = jnp.broadcast_to(own[:, 0:1], (nblk, wide))
    number = jnp.broadcast_to(own[:, 1:2], (nblk, wide))
    alive = jnp.broadcast_to(column[0:nblk, 2:3], (nblk, wide))
    before = lax.broadcasted_iota(jnp.int32, (nblk, nblk), 0) > lax.broadcasted_iota(jnp.int32, (nblk, nblk), 1)
    start = jnp.dot(before.astype(f32).astype(bf16), number.astype(bf16), preferred_element_type=f32)
    lane = lax.broadcasted_iota(jnp.int32, (nblk, wide), 1).astype(f32)
    block_of = lax.broadcasted_iota(jnp.int32, (nblk, wide), 0).astype(f32)
    here = (lane >= start) & (lane < start + number)
    particle = jnp.sum(jnp.where(here, block_of, 0.0), axis=0, keepdims=True)
    empty = 2.0 * half
    panel = empty + jnp.sum(jnp.where(here, first + lane - start - empty, 0.0), axis=0, keepdims=True)
    alive = jnp.sum(jnp.where(here, alive, 0.0), axis=0, keepdims=True)
    total = jnp.sum(number, axis=0, keepdims=True)
    row8 = rows8(wide)
    box[...] = jnp.where(row8 == 0, particle, jnp.where(row8 == 1, panel, jnp.where(row8 == 2, alive, total))).astype(jnp.int32)


def each_panel_block(panels, others, me, body):
    many = panels.shape[1] // BLK

    def run(ref, start):
        def one(k, carry):
            body(ref[:, block(k, BLK)], start + k)
            return carry

        lax.fori_loop(0, many, one, 0, unroll=8)

    run(panels, me * many)
    run(others, (1 - me) * many)
    for extra in range(WIN - 1):
        body(jnp.zeros((8, BLK), f32), 2 * many + extra)


def stack6(c1, c2, c3):
    pair = jnp.concatenate([c1, c2], axis=0).astype(bf16)
    return jnp.concatenate([pair, pair, jnp.concatenate([c3, c1], axis=0).astype(bf16)], axis=0)


def apart(a, b):
    none = jnp.zeros(a.shape, a.dtype)
    return jnp.concatenate([jnp.concatenate([a, none], axis=1), jnp.concatenate([none, b], axis=1)], axis=0)


TURN = (((0,), (0,)), ((), ()))


def panel_sums(
    counts, particles, panels, others, near, near_o, out, pan, box, v, vn, un, org, fe, geo, tot, column, items, sem
):
    me = lax.axis_index("panel")
    nblk = un.shape[0]
    list_pairs(near, near_o, counts, me, nblk, column, box)
    copy = pltpu.make_async_copy(box, items, sem)
    copy.start()
    particle_features(particles, un, fe, org)
    row = rows8(BLK)

    def build(p, at):
        pan[at] = p
        c = jnp.where(row < 3, p, 0.0)
        dist = jnp.where(row < 3, -2.0 * c, jnp.where(row < 6, up(c * c, 5), jnp.where(row == 6, 1.0, 0.0)))
        v[at] = stack6(*split3(dist))
        mn3 = jnp.where(row < 3, up(p, 3) * p[7:8, :], 0.0) * 3.0
        vn[at] = stack6(*split3(jnp.where(row < 3, -mn3, up(mn3 * c, 5))))
        geo[at, 0:8, :] = jnp.where(row < 2, up(p, 4), jnp.where(row == 2, up(p, 1), jnp.where(row < 6, -p, 0.0)))
        geo[at, 8:16, :] = jnp.where(row < 1, up(p, 5), jnp.where(row < 3, up(p, 2), 0.0))
        geo[at, 16:24, :] = jnp.where(row < 2, up(p, 1), jnp.where(row == 2, up(p, 6), 0.0))
        geo[at, 24:32, :] = jnp.where(row < 1, up(p, 2), jnp.where(row < 3, up(p, 7), 1.0))
        tot[at] = jnp.zeros((8, BLK), f32)

    each_panel_block(panels, others, me, build)
    copy.wait()
    filled = items[3, 0]
    lane = lax.broadcasted_iota(jnp.int32, (16, 2 * BLK), 1) % BLK

    def moments(n):
        qa, qb = items[0, n], items[0, n + 1]
        u = jnp.concatenate([un[qa], un[qb]], axis=0)
        r2 = lax.dot_general(u, apart(v[items[1, n]], v[items[1, n + 1]]), TURN, preferred_element_type=f32)
        inv = lax.rsqrt(r2)
        hi, lo = split2(inv * inv * inv)
        f = [fe[q] * jnp.where(lane < items[2, n + i], 1.0, 0.0).astype(bf16) for i, q in enumerate((qa, qb))]
        return jnp.concatenate(f, axis=0), jnp.concatenate([hi, lo], axis=0)

    def finish(n, g):
        q, at = items[0, n], items[1, n]
        m = geo[at, 0:8, :] * (geo[at, 24:32, :] - org[q, 16:24, :]) - geo[at, 8:16, :] * (geo[at, 16:24, :] - org[q, 8:16, :])
        tot[at] += (g[0:8] + g[8:16]) * m

    def some(i, carry):
        ns = [i * EACH1 + e for e in range(0, EACH1, 2)]
        parts = [moments(n) for n in ns]
        for n, (f, k) in zip(ns, parts):
            g = jnp.dot(f, k, preferred_element_type=f32)
            finish(n, g[0:16, 0:BLK])
            finish(n + 1, g[16:32, BLK:])
        return carry

    lax.fori_loop(0, (filled + EACH1 - 1) // EACH1, some, 0)
    for k in range(out.shape[1] // BLK):
        out[:, k * BLK : (k + 1) * BLK] = -inv_four_pi * jnp.sum(tot[k], axis=0, keepdims=True)


def share(rounds, part, parts):
    return jnp.minimum(rounds, (part * rounds + parts - 1) // parts)


def particle_sums(part, parts, pan, items, un, v, vn, org, *rest):
    row = rows8(BLK)
    total, = rest
    total[...] = jnp.zeros(total.shape, f32)
    listed = items[...]
    filled = listed[3, 0]
    def rows(n):
        p = pan[n[1]]
        d = jnp.where(row < 3, p - org[n[0], 0:8, :], jnp.where(row == 3, 1.0, 0.0))
        mn = jnp.where(row < 3, up(p, 3) * p[7:8], 0.0)
        d16, e16 = rows16(d), rows16(-p[6:7] * d - mn)
        return jnp.concatenate([d16, d16, e16, e16], axis=1)

    def factors(n, m):
        both = [jnp.concatenate([v[at], vn[at]], axis=1) for at in (n[1], m[1])]
        u = apart(un[n[0]], un[m[0]])
        pair = lax.dot_general(jnp.concatenate(both, axis=0), u, TURN, preferred_element_type=f32)
        inv = lax.rsqrt(pair[0:BLK])
        inv2 = inv * inv
        inv3 = inv2 * inv
        t1, t2 = split2(inv3 * (inv2 * pair[BLK:]))
        i1, i2 = split2(inv3)
        return jnp.concatenate([rows(n), rows(m)], axis=0), jnp.concatenate([t1, t2, i1, i2], axis=0)

    def finish(n, h):
        q = n[0]
        h = (h[0:8] + h[8:16]) * inv_four_pi
        total[q] += h - org[q, 24:32, :] * h[3:4]

    def some(i, carry):
        now = pltpu.roll(listed, listed.shape[1] - i * EACH, 1)
        ns = [(now[0, e], now[1, e]) for e in range(EACH)]
        parts = [factors(ns[e], ns[e + 1]) for e in range(0, EACH, 2)]
        for e, (f, k) in zip(range(0, EACH, 2), parts):
            h = jnp.dot(f, k, preferred_element_type=f32)
            finish(ns[e], h[0:16, 0:BLK])
            finish(ns[e + 1], h[16:32, BLK:])
        return carry

    rounds = (filled + EACH - 1) // EACH
    lax.fori_loop(share(rounds, part, parts), share(rounds, part + 1, parts), some, 0)


def last_sums(total, arrived, *rest):
    pieces, (normal, velocity) = rest[:-2], rest[-2:]
    half = normal.shape[1]
    me = lax.axis_index("panel")
    normal[...] = total[:, pl.ds(pl.multiple_of(me * half, half), half)] + arrived[...]
    for q in range(pieces[0].shape[0]):
        velocity[:, q * BLK : (q + 1) * BLK] = sum(p[q] for p in pieces)[0:3]


def vmem():
    return pl.BlockSpec(memory_space=pltpu.VMEM)


def smem():
    return pl.BlockSpec(memory_space=pltpu.SMEM)


def params(mib=24):
    return pltpu.CompilerParams(vmem_limit_bytes=mib * 1024 * 1024)


def fetch(source, out):
    out[0:6, :] = source[...]
    out[6:8, :] = jnp.zeros((2, out.shape[1]), f32)


def fetched(particles):
    return pl.pallas_call(
        fetch,
        out_shape=jax.ShapeDtypeStruct((8, particles.shape[1]), f32),
        in_specs=[vmem()],
        out_specs=vmem(),
        compiler_params=params(),
        name="fetch",
    )(particles)


def panel_side(counts, particles, panels, others, near, near_o):
    npan, width = 2 * panels.shape[1], particles.shape[1]
    nblk = width // BLK
    full = npan // BLK + WIN - 1
    wide = pl.cdiv(WIN * nblk + max(EACH1, EACH), BLK) * BLK
    return pl.pallas_call(
        panel_sums,
        out_shape=(
            jax.ShapeDtypeStruct((1, npan), f32),
            jax.ShapeDtypeStruct((full, 8, BLK), f32),
            jax.ShapeDtypeStruct((8, wide), jnp.int32),
            jax.ShapeDtypeStruct((full, 48, BLK), bf16),
            jax.ShapeDtypeStruct((full, 48, BLK), bf16),
            jax.ShapeDtypeStruct((nblk, 48, BLK), bf16),
            jax.ShapeDtypeStruct((nblk, 32, BLK), f32),
        ),
        in_specs=[vmem()] * 6,
        out_specs=(vmem(),) * 7,
        scratch_shapes=[
            pltpu.VMEM((nblk, 16, 2 * BLK), bf16),
            pltpu.VMEM((full, 32, BLK), f32),
            pltpu.VMEM((full, 8, BLK), f32),
            pltpu.VMEM((near.shape[1], 8), f32),
            pltpu.SMEM((8, wide), jnp.int32),
            pltpu.SemaphoreType.DMA,
        ],
        compiler_params=params(),
        name="panel_side",
    )(counts, particles, panels, others, near, near_o)


def particle_side(part, parts, pan, box, un, v, vn, org):
    return pl.pallas_call(
        functools.partial(particle_sums, part, parts),
        out_shape=jax.ShapeDtypeStruct((un.shape[0], 8, BLK), f32),
        in_specs=[vmem()] * 6,
        out_specs=vmem(),
        compiler_params=params(),
        cost_estimate=pl.CostEstimate(flops=10**9, bytes_accessed=10**5, transcendentals=0),
        name="particle_side",
    )(pan, box, un, v, vn, org)


def close(total, arrived, pieces):
    half = arrived.shape[0]
    normal, velocity = pl.pallas_call(
        last_sums,
        out_shape=(
            jax.ShapeDtypeStruct((1, half), f32),
            jax.ShapeDtypeStruct((3, pieces[0].shape[0] * BLK), f32),
        ),
        in_specs=[vmem()] * (2 + len(pieces)),
        out_specs=(vmem(), vmem()),
        compiler_params=params(),
        name="close",
    )(total.reshape(1, -1), arrived.reshape(1, -1), *pieces)
    return normal.reshape(half), velocity


def on_device(dom, panels, particles, counts, near):
    swap = [(0, 1), (1, 0)]
    others = lax.ppermute(panels, "panel", swap)
    near_o = lax.ppermute(near, "panel", swap)
    total, pan, box, v, vn, un, org = panel_side(counts.reshape(1, -1), fetched(particles), panels, others, near, near_o)
    total = total.reshape(total.shape[1])
    steps = [1 << b for b in range((dom - 1).bit_length())]
    parts = len(steps) + 1
    chunks = []

    for number, step in enumerate(steps):
        pairs = [(2 * i + c, 2 * (i ^ step) + 1 - c) for i in range(dom) for c in range(2)]
        total, at = lax.optimization_barrier((total, box))
        got = particle_side(number, parts, pan, at, un, v, vn, org)
        arrived, got = lax.optimization_barrier((lax.ppermute(total, ("dom", "panel"), pairs), got))
        chunks.append(got)
        total = total + arrived
    half = total.shape[0] // 2
    me = lax.axis_index("panel")
    total, at = lax.optimization_barrier((total, box))
    chunks.append(particle_side(parts - 1, parts, pan, at, un, v, vn, org))
    give = lax.dynamic_slice(total, ((1 - me) * half,), (half,))
    return close(total, lax.ppermute(give, "panel", swap), chunks)


def solution(mesh):
    return jax.shard_map(
        functools.partial(on_device, mesh.shape["dom"]),
        mesh=mesh,
        in_specs=(
            P(None, ("groups", "panel")),
            P(None, ("groups", "dom", "panel")),
            P(("groups", "dom", "panel")),
            P(("groups", "panel"), "dom"),
        ),
        out_specs=(P(("groups", "panel")), P(None, ("groups", "dom", "panel"))),
        check_vma=False,
    )
```
